32 devices in a mesh: region: 16 (over z, y, x), grp: 2 (over core).
Axes of the slice: x: 2, y: 2, z: 4, core: 2. Of those that a mesh axis runs over, the one named last changes fastest.
Arguments:
- node_feat: bfloat16 [65536, 256], P(('region', 'grp')), may hold values from -8 to 8
- edge_feat: bfloat16 [16, 524288], P(None, ('region', 'grp')), may hold values from -6 to 6
- edge_src: int32 [524288], P(('region', 'grp')), may hold values from 0 to 3071, as said below
- edge_dst: int32 [524288], P(('region', 'grp')), may hold values from 0 to 2047, as said below
- send_rows: int32 [32768], P(('region', 'grp')), may hold values from 0 to 2047, as said below
- node_count: int32 [32], P(('region', 'grp')), may hold values from 1024 to 2048
- edge_count: int32 [32], P(('region', 'grp')), may hold values from 8192 to 16384
- w_edge: bfloat16 [16, 256], replicated, may hold values from -1.5 to 1.5
- w_pre: bfloat16 [768, 256], replicated, may hold values from -0.375 to 0.375
- b_pre: float32 [256], replicated, may hold values from -3 to 3
- w_post_x: bfloat16 [256, 256], replicated, may hold values from -0.375 to 0.375
- w_post_agg: bfloat16 [768, 256], replicated, may hold values from -0.21875 to 0.21875
- w_lin: bfloat16 [256, 256], replicated, may hold values from -0.375 to 0.375
- norm_gain: float32 [256], replicated, may hold values from 0.1 to 1.9
- norm_bias: float32 [256], replicated, may hold values from -3 to 3
- out_grad: bfloat16 [65536, 256], P(('region', 'grp')), may hold values from -6 to 6
Outputs:
- output: bfloat16 [65536, 256], P(('region', 'grp'))
- node_grad: float32 [65536, 256], P(('region', 'grp'))
- w_edge_grad: float32 [16, 256], replicated
- w_pre_grad: float32 [768, 256], replicated
- b_pre_grad: float32 [256], replicated
- w_post_x_grad: float32 [256, 256], replicated
- w_post_agg_grad: float32 [768, 256], replicated
- w_lin_grad: float32 [256, 256], replicated
- gain_grad: float32 [256], replicated
- bias_grad: float32 [256], replicated
The draws below stay inside these ranges and needn't reach their ends.
Inputs may be any that keep to these rules, and one draw needn't show every extreme that they name: `edge_src`: index into the device's node table of 3072 rows; live edges name only live own rows, and halo rows from a neighbouring region only where that region exists. `edge_dst`: index among the device's own 2048 node rows; live edges name live rows. `send_rows`: each device's 1024 entries: 512 for the other half of its region, then 256 for the lower region, then 256 for the upper one; each names a live own row.
All inputs are finite; a program needn't handle non-finite values.
Results may differ from the reference program's by a relative error of at most 0.019.
The reference program's roundings to bfloat16 on the way count: a program that leaves them out, or rounds other values in their place, can miss the bound.
Values may be sent and summed in bfloat16 or wider, within the bound.
A program may use at most 320 MiB of HBM per device.

```python
import jax
import jax.numpy as jnp
from jax import lax

H = 256
ED = 16
TOWERS = 4
TW = 64
NODE_DEV = 2048
EDGE_DEV = 16384
SEND_PAIR = 512
SEND_SIDE = 256
SEND_DEV = 1024
EXT_DEV = 3072
NODES = 65536
EDGES = 524288
SENDS = 32768
N_REGION = 16
N_GRP = 2


def graph_counts(key):
    device_count = NODES // NODE_DEV
    node_key, edge_key = jax.random.split(key)
    node_live = jax.random.randint(node_key, (device_count,), NODE_DEV // 2, NODE_DEV + 1)
    edge_live = jax.random.randint(edge_key, (device_count,), EDGE_DEV // 2, EDGE_DEV + 1)
    node_live = node_live.at[0].set(NODE_DEV).at[device_count - 1].set(NODE_DEV // 2)
    edge_live = edge_live.at[0].set(EDGE_DEV).at[device_count - 1].set(EDGE_DEV // 2)
    return (node_live.astype(jnp.int32), edge_live.astype(jnp.int32))


def draw_node_count(key, part):
    node_live, edge_live = graph_counts(key)
    return node_live


def draw_edge_count(key, part):
    node_live, edge_live = graph_counts(key)
    return edge_live


def draw_edge_dst(key, part):
    node_live, edge_live = graph_counts(key)
    key = jax.random.fold_in(key, 7)
    device_of = jnp.arange(EDGES) // EDGE_DEV
    target = jax.random.randint(key, (EDGES,), 0, node_live[device_of])
    target = target.at[0].set(NODE_DEV - 1).at[1].set(0)
    return target.astype(jnp.int32)


def draw_edge_src(key, part):
    node_live, edge_live = graph_counts(key)
    key = jax.random.fold_in(key, 9)
    kind_key, own_key, halo_key = jax.random.split(key, 3)
    device_of = jnp.arange(EDGES) // EDGE_DEV
    region_of = device_of // N_GRP
    kind = jax.random.randint(kind_key, (EDGES,), 0, 4)
    kind = jnp.where((kind == 2) & (region_of == 0), 0, kind)
    kind = jnp.where((kind == 3) & (region_of == N_REGION - 1), 0, kind)
    own = jax.random.randint(own_key, (EDGES,), 0, node_live[device_of])
    halo_pick = jax.random.randint(halo_key, (EDGES,), 0, SEND_PAIR)
    side_pick = halo_pick % SEND_SIDE
    pair = NODE_DEV + halo_pick
    lower = NODE_DEV + SEND_PAIR + side_pick
    upper = NODE_DEV + SEND_PAIR + SEND_SIDE + side_pick
    source = jnp.where(kind == 0, own, jnp.where(kind == 1, pair, jnp.where(kind == 2, lower, upper)))
    source = source.at[2].set(EXT_DEV - 1).at[3].set(0)
    return source.astype(jnp.int32)


def draw_send_rows(key, part):
    node_live, edge_live = graph_counts(key)
    key = jax.random.fold_in(key, 13)
    device_of = jnp.arange(SENDS) // SEND_DEV
    rows = jax.random.randint(key, (SENDS,), 0, node_live[device_of])
    rows = rows.at[0].set(NODE_DEV - 1).at[1].set(0)
    return rows.astype(jnp.int32)


def draw_node_feat(key, part):
    key = jax.random.fold_in(key, 11)
    value_key, scale_key = jax.random.split(key)
    device_count = NODES // NODE_DEV
    position = (jnp.arange(NODES) // NODE_DEV).astype(jnp.float32) / max(device_count - 1, 1)
    row_scale = jnp.exp(jax.random.uniform(scale_key, (NODES, 1), jnp.float32, -0.5, 0.5))
    ramp = 0.3 * 3.0 ** position
    values = jax.random.normal(value_key, (NODES, H), jnp.float32)
    return jnp.clip(values * ramp[:, None] * row_scale, -8.0, 8.0).astype(jnp.bfloat16)


def steps_of(rng, shape, pieces, least, top_value):
    def one(dim, shards_of):
        heights = jax.random.uniform(jax.random.fold_in(jax.random.fold_in(rng, 6), dim), (shards_of,), jnp.float32, least / len(pieces), top_value / len(pieces))
        return jnp.repeat(jnp.exp(heights), shape[dim] // shards_of).reshape((-1,) + (1,) * (len(shape) - dim - 1))

    gain = one(*pieces[0])
    for cut in pieces[1:]:
        gain = gain * one(*cut)
    return gain


def scatter_about(key, extent, deviation, bound, shards=(), kind=jnp.bfloat16):
    gain = steps_of(key, extent, shards, -0.22, 0.18) if shards else 1.0
    result = jax.random.normal(key, extent, jnp.float32) * deviation * gain
    return jnp.minimum(jnp.maximum(result, -bound), bound).astype(kind)


def setup_inputs(seed: int = 0) -> dict:
    streams_of = jax.random.split(jax.random.key(seed), 17)
    return {
        "node_feat": draw_node_feat(jax.random.fold_in(streams_of[16], 71), 0),
        "edge_feat": scatter_about(streams_of[1], (ED, EDGES), 1.0, 6.0, ((1, 32),)),
        "edge_src": draw_edge_src(jax.random.fold_in(streams_of[16], 71), 0),
        "edge_dst": draw_edge_dst(jax.random.fold_in(streams_of[16], 71), 0),
        "send_rows": draw_send_rows(jax.random.fold_in(streams_of[16], 71), 0),
        "node_count": draw_node_count(jax.random.fold_in(streams_of[16], 71), 0),
        "edge_count": draw_edge_count(jax.random.fold_in(streams_of[16], 71), 0),
        "w_edge": scatter_about(streams_of[7], (ED, H), ED ** -0.5, 1.5),
        "w_pre": scatter_about(streams_of[8], (3 * H, H), H ** -0.5, 0.375),
        "b_pre": scatter_about(streams_of[9], (H,), 0.5, 3.0, (), jnp.float32),
        "w_post_x": scatter_about(streams_of[10], (H, H), H ** -0.5, 0.375),
        "w_post_agg": scatter_about(streams_of[11], (12 * TW, H), (12 * TW) ** -0.5, 0.21875),
        "w_lin": scatter_about(streams_of[12], (H, H), H ** -0.5, 0.375),
        "norm_gain": jnp.clip(1.0 + 0.18 * jax.random.normal(streams_of[13], (H,), jnp.float32), 0.1, 1.9),
        "norm_bias": scatter_about(streams_of[14], (H,), 0.5, 3.0, (), jnp.float32),
        "out_grad": scatter_about(streams_of[15], (NODES, H), 1.0, 6.0, ((0, 32),)),
    }


avg_log_degree = 2.2
norm_eps = 1e-05

@jax.custom_vjp
def low(v):
    return lax.optimization_barrier(v.astype(jnp.bfloat16)).astype(jnp.float32)

@jax.custom_vjp
def low_back(v):
    return v

def low_keep(v):
    return (low(v), None)

def low_pass(kept, grad):
    return (grad,)

def back_keep(v):
    return (v, None)

def back_low(kept, grad):
    return (low(grad),)
low.defvjp(low_keep, low_pass)
low_back.defvjp(back_keep, back_low)

def matmul(left, right):
    return jnp.dot(left, right, precision=lax.Precision.HIGHEST)

def halo_index(send_rows):
    device_count = NODES // NODE_DEV
    lists = send_rows.reshape(device_count, SEND_DEV)
    device_ids = jnp.arange(device_count, dtype=jnp.int32)
    region_ids = device_ids // N_GRP
    partner = device_ids + 1 - 2 * (device_ids % N_GRP)
    lower_dev = jnp.maximum(device_ids - N_GRP, 0)
    upper_dev = jnp.minimum(device_ids + N_GRP, device_count - 1)
    own_rows = device_ids[:, None] * NODE_DEV + jnp.arange(NODE_DEV, dtype=jnp.int32)[None, :]
    pair_rows = partner[:, None] * NODE_DEV + lists[partner, :SEND_PAIR]
    lower_rows = lower_dev[:, None] * NODE_DEV + lists[lower_dev, SEND_PAIR + SEND_SIDE:]
    upper_rows = upper_dev[:, None] * NODE_DEV + lists[upper_dev, SEND_PAIR:SEND_PAIR + SEND_SIDE]
    index = jnp.concatenate([own_rows, pair_rows, lower_rows, upper_rows], 1).astype(jnp.int32)
    lower_ok = jnp.broadcast_to((region_ids > 0)[:, None], (device_count, SEND_SIDE))
    upper_ok = jnp.broadcast_to((region_ids < N_REGION - 1)[:, None], (device_count, SEND_SIDE))
    always = jnp.ones((device_count, NODE_DEV + SEND_PAIR), dtype=bool)
    valid = jnp.concatenate([always, lower_ok, upper_ok], 1).astype(jnp.float32)
    return (index, valid)

def reference(node_feat, edge_feat, edge_src, edge_dst, send_rows, node_count, edge_count, w_edge, w_pre, b_pre, w_post_x, w_post_agg, w_lin, norm_gain, norm_bias, out_grad):
    device_count = NODES // NODE_DEV
    index, valid = halo_index(send_rows)
    src_blocks = edge_src.reshape(device_count, EDGE_DEV)
    dst_blocks = edge_dst.reshape(device_count, EDGE_DEV)
    node_mask = (jnp.arange(NODE_DEV, dtype=jnp.int32)[None, :] < node_count[:, None]).astype(jnp.float32).reshape(NODES, 1)

    def forward(feat, edge_in, w_edge, w_pre, b_pre, w_post_x, w_post_agg, w_lin, norm_gain, norm_bias):
        tables = feat[index] * valid[:, :, None]
        edge_blocks = jnp.transpose(edge_in.reshape(ED, device_count, EDGE_DEV), (1, 0, 2))

        def one_block(items):
            table, edge_block, source, target, node_live, edge_live = items
            own = table[:NODE_DEV]
            edge_mask = (jnp.arange(EDGE_DEV, dtype=jnp.int32) < edge_live).astype(jnp.float32)[:, None]
            embed = low(low_back(matmul(edge_block.T, w_edge)))
            dst_part = low_back(matmul(own, w_pre[:H]))
            src_part = low_back(matmul(table, w_pre[H:2 * H]))
            summed = dst_part[target] + src_part[source] + matmul(embed, w_pre[2 * H:]) + b_pre
            messages = low_back(summed)

            def by_target(values):
                return jax.ops.segment_sum(values, target, num_segments=NODE_DEV)
            degree = by_target(edge_mask[:, 0])[:, None]
            clamped = jnp.maximum(degree, 1.0)
            mean_value = by_target(edge_mask * messages) / clamped
            centred = messages - mean_value[target]
            spread = jnp.sqrt(by_target(edge_mask * centred * centred) / clamped + 1.0)
            up_total = by_target(edge_mask * jnp.exp(messages)) + 1.0
            down_total = by_target(edge_mask * jnp.exp(-messages)) + 1.0
            log_count = jnp.log(degree + 1.0)
            soft_max = jnp.log(up_total) - log_count
            soft_min = log_count - jnp.log(down_total)
            amplify = log_count / avg_log_degree
            attenuate = avg_log_degree / jnp.log(clamped + 1.0)
            stacked = jnp.stack([mean_value, soft_max, soft_min, spread], 1)
            features = jnp.concatenate([stacked, stacked * amplify[:, :, None], stacked * attenuate[:, :, None]], 1)
            feat_low = low(features).reshape(NODE_DEV, 12, TOWERS, TW)
            tower_weight = w_post_agg.reshape(12, TW, TOWERS, TW)
            tower_out = jnp.einsum('ngtc,gcto->nto', feat_low, tower_weight, precision=lax.Precision.HIGHEST).reshape(NODE_DEV, H)
            post_value = low(low_back(matmul(own, w_post_x) + tower_out))
            return low_back(matmul(post_value, w_lin))
        lin_all = lax.map(jax.checkpoint(one_block), (tables, edge_blocks, src_blocks, dst_blocks, node_count, edge_count))
        lin_out = lin_all.reshape(NODES, H)
        count_all = jnp.sum(node_mask)
        centre = lax.optimization_barrier(jnp.sum(node_mask * lin_out, 0)) / count_all
        variance = lax.optimization_barrier(jnp.sum(node_mask * lin_out * lin_out, 0)) / count_all - centre * centre
        normed = (lin_out - centre) * lax.rsqrt(variance + norm_eps)
        shifted = normed * norm_gain + norm_bias
        return feat + node_mask * jax.nn.gelu(shifted)
    primals = (node_feat.astype(jnp.float32), edge_feat.astype(jnp.float32), w_edge.astype(jnp.float32), w_pre.astype(jnp.float32), b_pre, w_post_x.astype(jnp.float32), w_post_agg.astype(jnp.float32), w_lin.astype(jnp.float32), norm_gain, norm_bias)
    output, back = jax.vjp(forward, *primals)
    grads = back(out_grad.astype(jnp.float32))
    return (output.astype(jnp.bfloat16), grads[0], grads[2], grads[3], grads[4], grads[5], grads[6], grads[7], grads[8], grads[9])
```

```python
import functools
import jax
import jax.numpy as jnp
from jax import lax
from jax.experimental import pallas as pl
from jax.experimental.pallas import tpu as pltpu
from jax.sharding import PartitionSpec as P

TOWERS = 4
SUB = 512
WIN = 128
LANES = 128
ROWS_EL = 1024
bf16 = jnp.bfloat16
f32 = jnp.float32
i32 = jnp.int32
VMEM = pl.BlockSpec(memory_space=pltpu.VMEM)
SMEM = pl.BlockSpec(memory_space=pltpu.SMEM)


def params(**kw):
    return pltpu.CompilerParams(vmem_limit_bytes=60 * 2**20, **kw)


def dot(a, b):
    return jnp.dot(a, b, preferred_element_type=f32)


def dot_nt(a, b):
    return lax.dot_general(a, b, (((1,), (1,)), ((), ())), preferred_element_type=f32)


def dot_tn(a, b):
    return lax.dot_general(a, b, (((0,), (0,)), ((), ())), preferred_element_type=f32)


def bitonic(key, pay):
    n = LANES
    regs = key.shape[0] // 8
    sub_bits, reg_bits = 3, regs.bit_length() - 1
    low_bits = sub_bits + reg_bits
    total = low_bits + 7
    keys = [key[8 * v : 8 * v + 8] for v in range(regs)]
    pays = [pay[8 * v : 8 * v + 8] for v in range(regs)]
    sub = lax.broadcasted_iota(i32, (8, n), 0)
    lane = lax.broadcasted_iota(i32, (8, n), 1)

    def bit_of(b, v):
        if b < sub_bits:
            return ((sub >> b) & 1) == 1
        if b < low_bits:
            return bool((v >> (b - sub_bits)) & 1)
        if b < total:
            return ((lane >> (b - low_bits)) & 1) == 1
        return False

    def flip(mask, by):
        if isinstance(by, bool):
            return jnp.logical_not(mask) if by else mask
        return jnp.logical_xor(mask, by)

    for k in range(total):
        for j in range(k, -1, -1):
            if sub_bits <= j < low_bits:
                d = 1 << (j - sub_bits)
                for v in range(regs):
                    if v & d:
                        continue
                    w = v | d
                    a, b, pa, pb = keys[v], keys[w], pays[v], pays[w]
                    swap = flip(a > b, bit_of(k + 1, v))
                    keys[v], keys[w] = jnp.where(swap, b, a), jnp.where(swap, a, b)
                    pays[v], pays[w] = jnp.where(swap, pb, pa), jnp.where(swap, pa, pb)
                continue
            if j < sub_bits:
                d, axis, size = 1 << j, 0, 8
            else:
                d, axis, size = 1 << (j - low_bits), 1, n
            bit = bit_of(j, 0)

            def partner(x):
                up = pltpu.roll(x, d, axis)
                if 2 * d == size:
                    return up
                return jnp.where(bit, up, pltpu.roll(x, size - d, axis))

            for v in range(regs):
                a, pa = keys[v], pays[v]
                b, pb = partner(a), partner(pa)
                take = jnp.logical_xor(a > b, flip(bit, bit_of(k + 1, v)))
                keys[v], pays[v] = jnp.where(take, b, a), jnp.where(take, pb, pa)
    return jnp.concatenate(keys, 0), jnp.concatenate(pays, 0)


def sort_kernel(nodes, count, dst, src, perm_col, dst_col, dst_row, dst_idx, src_idx):
    rows = dst.shape[0]
    place = lax.broadcasted_iota(i32, (rows, LANES), 0) * LANES + lax.broadcasted_iota(
        i32, (rows, LANES), 1
    )
    total = rows * LANES
    shift = total.bit_length() - 1
    target = jnp.where(place < count[0], dst[...], nodes)
    key, pay = bitonic((target << shift) | place, src[...])
    perm_col[...] = key & (total - 1)
    target = key >> shift
    dst_col[...] = target
    row = target.T
    dst_row[...] = row
    dst_idx[...] = 2 * jnp.minimum(row, nodes - 1)
    src_idx[...] = 2 * pay.T


def sort_edges(edge_dst, edge_src, edge_count, nodes):
    rows = edge_dst.shape[0] // LANES
    shape = jax.ShapeDtypeStruct((rows, LANES), i32)
    return pl.pallas_call(
        functools.partial(sort_kernel, nodes),
        out_shape=[shape] * 5,
        in_specs=[SMEM, VMEM, VMEM],
        out_specs=[VMEM] * 5,
        compiler_params=params(),
        name="sort_edges",
    )(edge_count, edge_dst.reshape(rows, LANES), edge_src.reshape(rows, LANES))


def flat(ref):
    n, s, l = ref.shape
    return ref.reshape(n * s, l)


def put_rows(ref, start, value):
    n = value.shape[0]
    for j in range(2):
        flat(ref)[pl.ds(2 * start + j, n, stride=2), :] = value[:, j * LANES : (j + 1) * LANES]


def get_rows(ref, n):
    return jnp.concatenate([flat(ref)[pl.ds(j, n, stride=2), :] for j in range(2)], 1)


def columns_of(col_ref, first):
    turned = pltpu.roll(col_ref[...], (LANES - first) & (LANES - 1), 1)
    return [turned[:, c : c + 1] for c in range(SUB // LANES)]


def i16(x):
    return x.astype(jnp.int16)


ONE = 1.0


def onehot(match):
    return jnp.where(match, jnp.array(1, bf16), jnp.array(0, bf16))


def window_of(dst_idx, row):
    first = dst_idx[row, 0] >> 1
    last = dst_idx[row + SUB // LANES - 1, LANES - 1] >> 1
    base = (first >> 4) << 4
    return base, ((last - base) >> (WIN.bit_length() - 1)) + 1


def target_rows(dst_row, block, base):
    iota = lax.broadcasted_iota(jnp.int16, (WIN, LANES), 0)
    parts = []
    for c in range(SUB // LANES):
        rel = i16(jnp.broadcast_to(dst_row[block, c : c + 1, :] - base, (WIN, LANES)))
        parts.append(onehot(rel == iota))
    return parts


def forward_kernel(
    src_idx,
    dst_idx,
    edge_live,
    table,
    spread_feat,
    perm_col,
    dst_row,
    w_pre,
    w_edge_rep,
    b_pre,
    m_out,
    feat_out,
    acc,
    deg,
    src_part,
    dst_part,
    rows_a,
    rows_b,
    pick,
    vals,
):
    step = pl.program_id(0)
    steps = pl.num_programs(0)
    per_step = m_out.shape[0]
    subs = per_step // SUB
    lines = SUB // LANES
    hidden = w_pre.shape[1]
    nodes = dst_part.shape[0]
    bufs = [rows_a, rows_b]

    def gather(block, into):
        for j in range(SUB):
            r, c = block * lines + j // LANES, j % LANES
            flat(into)[pl.ds(2 * j, 2), :] = (
                flat(src_part)[pl.ds(src_idx[r, c], 2), :]
                + flat(dst_part)[pl.ds(dst_idx[r, c], 2), :]
            )

    @pl.when(step == 0)
    def _():
        acc[...] = jnp.zeros_like(acc)
        deg[...] = jnp.zeros_like(deg)

        @pl.loop(0, table.shape[0] // 256)
        def _(c):
            at = pl.multiple_of(c * 256, 256)
            put_rows(src_part, at, dot(table[pl.ds(at, 256), :], w_pre[hidden : 2 * hidden, :]))

        @pl.loop(0, nodes // 256)
        def _(c):
            at = pl.multiple_of(c * 256, 256)
            put_rows(dst_part, at, dot(table[pl.ds(at, 256), :], w_pre[:hidden, :]))

        gather(0, rows_a)

    def add_window(base, at):
        hot = target_rows(dst_row, at, base)
        total = hot[0].astype(f32)
        for h in hot[1:]:
            total = total + h.astype(f32)
        here = pl.ds(pl.multiple_of(base, 8), WIN)
        deg[here, :] += total
        hot = jnp.concatenate(hot, 1)
        acc[here, :hidden] += dot(hot, vals[:, :hidden])
        acc[here, hidden : 2 * hidden] += dot(hot, vals[:, hidden : 2 * hidden]) + dot(
            hot, vals[:, 2 * hidden : 3 * hidden]
        )
        acc[here, 2 * hidden :] += dot(hot, vals[:, 3 * hidden :])

    for s in range(subs):
        block = step * subs + s
        following = jnp.where(block + 1 < steps * subs, block + 1, 0)
        gather(following, bufs[(s + 1) % 2])
        wide = lax.broadcasted_iota(jnp.int16, (LANES, LANES), 1)
        highs = []
        for c, place in enumerate(columns_of(perm_col, block * lines)):
            low = i16(jnp.broadcast_to(place & (ROWS_EL - 1), (LANES, LANES)))
            highs.append(jnp.broadcast_to(place >> (ROWS_EL.bit_length() - 1), (LANES, hidden)))
            for t in range(ROWS_EL // LANES):
                pick[c * LANES : (c + 1) * LANES, t * LANES : (t + 1) * LANES] = onehot(
                    low == wide + jnp.int16(t * LANES)
                )
        found = dot(pick[...], spread_feat[...])
        high = jnp.concatenate(highs, 0)
        lane = lax.broadcasted_iota(i32, (SUB, hidden), 1)
        found = jnp.where((lane & 15) == high, found, 0.0).astype(bf16)
        select = lax.broadcasted_iota(i32, (16, hidden), 1) >> 4
        select = onehot(select == lax.broadcasted_iota(i32, (16, hidden), 0))
        feat_out[:, s * SUB : (s + 1) * SUB] = dot_nt(select, found).astype(bf16)
        embed = dot(found, w_edge_rep[...]).astype(bf16)
        m = get_rows(bufs[s % 2], SUB) + dot(embed, w_pre[2 * hidden :, :]) + b_pre[...]
        spot = lax.broadcasted_iota(i32, (SUB, hidden), 0) + block * SUB
        m = jnp.where(spot < edge_live[0], m, 0.0)
        m_out[s * SUB : (s + 1) * SUB, :] = m
        low = m.astype(bf16)
        vals[:, :hidden] = low
        wide_low = low.astype(f32)
        square = wide_low * wide_low
        top = square.astype(bf16)
        vals[:, hidden : 2 * hidden] = top
        vals[:, 2 * hidden : 3 * hidden] = (square - top.astype(f32)).astype(bf16)
        vals[:, 3 * hidden : 4 * hidden] = jnp.exp(m).astype(bf16)
        vals[:, 4 * hidden :] = jnp.exp(-m).astype(bf16)
        base, windows = window_of(dst_idx, block * lines)
        add_window(base, block)

        @pl.loop(1, windows)
        def _(w):
            add_window(base + w * WIN, block)


def forward_edges(sorted_edges, edge_count, table, edge_feat, w_edge, w_pre, b_pre, nodes):
    perm_col, dst_col, dst_row, dst_idx, src_idx = sorted_edges
    edges = edge_feat.shape[1]
    hidden = w_pre.shape[1]
    ext = table.shape[0]
    spread_feat = edge_feat.reshape(-1, ROWS_EL).T
    w_edge_rep = jnp.repeat(w_edge, edges // ROWS_EL, axis=0)
    step_edges = 1024
    steps = edges // step_edges
    whole = lambda *shape: pl.BlockSpec(shape, lambda i: (0,) * len(shape))
    return pl.pallas_call(
        forward_kernel,
        grid=(steps,),
        out_shape=[
            jax.ShapeDtypeStruct((edges, hidden), f32),
            jax.ShapeDtypeStruct((16, edges), bf16),
            jax.ShapeDtypeStruct((nodes + WIN, 4 * hidden), f32),
            jax.ShapeDtypeStruct((nodes + WIN, LANES), f32),
        ],
        in_specs=[
            SMEM,
            SMEM,
            SMEM,
            whole(ext, hidden),
            whole(ROWS_EL, hidden),
            whole(LANES, LANES),
            whole(edges // SUB, SUB // LANES, LANES),
            whole(3 * hidden, hidden),
            whole(hidden, hidden),
            whole(1, hidden),
        ],
        out_specs=[
            pl.BlockSpec((step_edges, hidden), lambda i: (i, 0)),
            pl.BlockSpec((16, step_edges), lambda i: (0, i)),
            whole(nodes + WIN, 4 * hidden),
            whole(nodes + WIN, LANES),
        ],
        scratch_shapes=[
            pltpu.VMEM((ext, 2, LANES), f32),
            pltpu.VMEM((nodes, 2, LANES), f32),
            pltpu.VMEM((SUB, 2, LANES), f32),
            pltpu.VMEM((SUB, 2, LANES), f32),
            pltpu.VMEM((SUB, ROWS_EL), bf16),
            pltpu.VMEM((SUB, 5 * hidden), bf16),
        ],
        compiler_params=params(),
        name="forward_edges",
    )(
        src_idx,
        dst_idx,
        edge_count,
        table,
        spread_feat,
        perm_col,
        dst_row.reshape(edges // SUB, SUB // LANES, LANES),
        w_pre,
        w_edge_rep,
        b_pre.reshape(1, hidden),
    )


CHAINS = 4


def backward_kernel(
    src_idx,
    dst_idx,
    m_in,
    feat,
    dst_col,
    dst_row,
    weights,
    dst_sum,
    src_sum,
    feat_sum,
    acc0,
    acc1,
    acc2,
    acc3,
    rows_a,
    rows_b,
    got,
    low,
):
    step = pl.program_id(0)
    steps = pl.num_programs(0)
    subs = m_in.shape[0] // SUB
    lines = SUB // LANES
    hidden = m_in.shape[1]
    accs = [acc0, acc1, acc2, acc3]
    bufs = [rows_a, rows_b]

    @pl.when(step == 0)
    def _():
        for ref in accs + bufs:
            ref[...] = jnp.zeros_like(ref)
        dst_sum[...] = jnp.zeros_like(dst_sum)
        feat_sum[...] = jnp.zeros_like(feat_sum)

    def scatter(block, rows):
        for j in range(SUB):
            into = flat(accs[j % CHAINS])
            at = pl.ds(src_idx[block * lines + j // LANES, j % LANES], 2)
            into[at, :] = into[at, :] + flat(rows)[pl.ds(2 * j, 2), :]

    def take_window(block, base, more):
        wide = lax.broadcasted_iota(jnp.int16, (LANES, WIN), 1)
        hot = []
        for place in columns_of(dst_col, block * lines):
            hot.append(onehot(i16(jnp.broadcast_to(place - base, (LANES, WIN))) == wide))
        hot = jnp.concatenate(hot, 0)
        here = pl.ds(pl.multiple_of(base, 16), WIN)
        for q in range(4):
            part = dot(hot, weights[here, q * hidden : (q + 1) * hidden])
            if q == 0:
                part = part + dot(hot, weights[here, 4 * hidden :])
            to = slice(q * hidden, (q + 1) * hidden)
            got[:, to] = got[:, to] + part if more else part

    def add_window(block, base):
        hot = jnp.concatenate(target_rows(dst_row, block, base), 1)
        dst_sum[pl.ds(pl.multiple_of(base, 8), WIN), :] += dot(hot, low[...])

    for s in range(subs):
        block = step * subs + s
        scatter(jnp.maximum(block - 1, 0), bufs[(s + 1) % 2])
        base, windows = window_of(dst_idx, block * lines)
        take_window(block, base, False)

        @pl.loop(1, windows)
        def _(w):
            take_window(block, base + w * WIN, True)

        m = m_in[s * SUB : (s + 1) * SUB, :]
        grad = (
            got[:, :hidden]
            + got[:, hidden : 2 * hidden] * m
            + got[:, 2 * hidden : 3 * hidden] * jnp.exp(m)
            + got[:, 3 * hidden : 4 * hidden] * jnp.exp(-m)
        ).astype(bf16)
        low[...] = grad
        put_rows(bufs[s % 2], 0, grad.astype(f32))
        feat_sum[...] += dot(feat[:, s * SUB : (s + 1) * SUB], low[...])
        add_window(block, base)

        @pl.loop(1, windows)
        def _(w):
            add_window(block, base + w * WIN)

    @pl.when(step == steps - 1)
    def _():
        scatter(steps * subs - 1, bufs[(subs - 1) % 2])

        @pl.loop(0, src_sum.shape[0] // 256)
        def _(c):
            at = pl.multiple_of(c * 256, 256)
            for j in range(2):
                here = pl.ds(2 * at + j, 256, stride=2)
                src_sum[pl.ds(at, 256), j * LANES : (j + 1) * LANES] = (
                    flat(acc0)[here, :] + flat(acc1)[here, :]
                ) + (flat(acc2)[here, :] + flat(acc3)[here, :])


def backward_edges(sorted_edges, messages, feat, weights, ext):
    perm_col, dst_col, dst_row, dst_idx, src_idx = sorted_edges
    edges, hidden = messages.shape
    padded = weights.shape[0]
    step_edges = 2 * SUB
    whole = lambda *shape: pl.BlockSpec(shape, lambda i: (0,) * len(shape))
    return pl.pallas_call(
        backward_kernel,
        grid=(edges // step_edges,),
        out_shape=[
            jax.ShapeDtypeStruct((padded, hidden), f32),
            jax.ShapeDtypeStruct((ext, hidden), f32),
            jax.ShapeDtypeStruct((16, hidden), f32),
        ],
        in_specs=[
            SMEM,
            SMEM,
            pl.BlockSpec((step_edges, hidden), lambda i: (i, 0)),
            pl.BlockSpec((16, step_edges), lambda i: (0, i)),
            whole(LANES, LANES),
            whole(edges // SUB, SUB // LANES, LANES),
            whole(padded, 5 * hidden),
        ],
        out_specs=[whole(padded, hidden), whole(ext, hidden), whole(16, hidden)],
        scratch_shapes=[pltpu.VMEM((ext, 2, LANES), f32)] * CHAINS
        + [pltpu.VMEM((SUB, 2, LANES), f32)] * 2
        + [pltpu.VMEM((SUB, 4 * hidden), f32), pltpu.VMEM((SUB, hidden), bf16)],
        compiler_params=params(),
        name="backward_edges",
    )(
        src_idx,
        dst_idx,
        messages,
        feat,
        dst_col,
        dst_row.reshape(edges // SUB, SUB // LANES, LANES),
        weights,
    )


avg_log_degree = 2.2
norm_eps = 1e-05


def from_partner(block, axis, stride):
    count = lax.axis_size(axis)
    route = []
    for low in range(count):
        high = low | 1 << stride
        if high != low and high < count:
            route += [(low, high), (high, low)]
    return lax.ppermute(block, axis, route)


def passed_along(value, axis, steps):
    count = lax.axis_size(axis)
    first, last = (max(0, -steps), min(count, count - steps))
    return lax.ppermute(value, axis, [(source, source + steps) for source in range(first, last)])


def per_device(
    node_feat,
    edge_feat,
    edge_src,
    edge_dst,
    send_rows,
    node_count,
    edge_count,
    w_edge,
    w_pre,
    b_pre,
    w_post_x,
    w_post_agg,
    w_lin,
    norm_gain,
    norm_bias,
    out_grad,
):
    nodes, hidden = node_feat.shape
    pair_size, side_size = nodes // 4, nodes // 8
    tower_width = hidden // TOWERS
    node_mask = (jnp.arange(nodes) < node_count[0]).astype(f32)[:, None]
    sent = jnp.take(node_feat, send_rows, axis=0)
    pair_in = from_partner(sent[:pair_size], "grp", 0)
    from_lower = passed_along(sent[pair_size + side_size :], "region", 1)
    from_upper = passed_along(sent[pair_size : pair_size + side_size], "region", -1)
    table = jnp.concatenate([node_feat, pair_in, from_lower, from_upper], 0)
    w_dst, w_src, w_edg = w_pre[:hidden], w_pre[hidden : 2 * hidden], w_pre[2 * hidden :]

    order = sort_edges(edge_dst, edge_src, edge_count, nodes)
    messages, feat, acc, deg = forward_edges(
        order, edge_count, table, edge_feat, w_edge, w_pre, b_pre, nodes
    )
    acc = acc[:nodes]
    degree = jnp.sum(deg[:nodes], 1, keepdims=True)
    clamped = jnp.maximum(degree, 1.0)
    mean_value = acc[:, :hidden] / clamped
    spread = jnp.sqrt(
        jnp.maximum(acc[:, hidden : 2 * hidden] / clamped - mean_value * mean_value, 0.0) + 1.0
    )
    up_total = acc[:, 2 * hidden : 3 * hidden] + 1.0
    down_total = acc[:, 3 * hidden :] + 1.0
    log_count = jnp.log(degree + 1.0)
    soft_max = jnp.log(up_total) - log_count
    soft_min = log_count - jnp.log(down_total)
    amplify = log_count / avg_log_degree
    attenuate = avg_log_degree / jnp.log(clamped + 1.0)
    stacked = jnp.concatenate([mean_value, soft_max, soft_min, spread], 1)
    features = jnp.concatenate([stacked, stacked * amplify, stacked * attenuate], 1)
    feat_low = features.astype(bf16).reshape(nodes, 12, TOWERS, tower_width)
    tower_weight = w_post_agg.reshape(12, tower_width, TOWERS, tower_width)
    tower_out = jnp.einsum(
        "ngtc,gcto->nto", feat_low, tower_weight, preferred_element_type=f32
    ).reshape(nodes, hidden)
    post_value = (dot(node_feat, w_post_x) + tower_out).astype(bf16)
    lin_out = dot(post_value, w_lin)
    both = ("region", "grp")
    count_all, first_sum, second_sum = lax.psum(
        (
            jnp.sum(node_mask),
            jnp.sum(node_mask * lin_out, 0),
            jnp.sum(node_mask * lin_out * lin_out, 0),
        ),
        both,
    )
    centre = first_sum / count_all
    inverse = lax.rsqrt(second_sum / count_all - centre * centre + norm_eps)
    normed = (lin_out - centre) * inverse
    shifted = normed * norm_gain + norm_bias
    activated, gelu_back = jax.vjp(jax.nn.gelu, shifted)
    output = (node_feat.astype(f32) + node_mask * activated).astype(bf16)
    upstream = out_grad.astype(f32)
    (shift_grad,) = gelu_back(upstream * node_mask)
    bias_grad, gain_grad = lax.psum(
        (jnp.sum(shift_grad, 0), jnp.sum(shift_grad * normed, 0)), both
    )
    lin_grad = (
        node_mask
        * inverse
        * norm_gain
        * (shift_grad - bias_grad / count_all - normed * (gain_grad / count_all))
    ).astype(bf16)
    w_lin_grad = dot_tn(post_value, lin_grad)
    post_grad = dot_nt(lin_grad, w_lin).astype(bf16)
    w_post_x_grad = dot_tn(node_feat, post_grad)
    input_grad = upstream + dot_nt(post_grad, w_post_x)
    post_split = post_grad.reshape(nodes, TOWERS, tower_width)
    w_post_agg_grad = jnp.einsum(
        "ngtc,nto->gcto", feat_low, post_split, preferred_element_type=f32
    ).reshape(12 * tower_width, hidden)
    feature_grad = jnp.einsum(
        "nto,gcto->ngtc", post_split, tower_weight, preferred_element_type=f32
    ).reshape(nodes, 3, 4, hidden)
    agg_grad = (
        feature_grad[:, 0]
        + amplify[:, :, None] * feature_grad[:, 1]
        + attenuate[:, :, None] * feature_grad[:, 2]
    )
    weight_spread = (agg_grad[:, 3] / (spread * clamped)).astype(bf16)
    weight_mean = agg_grad[:, 0] / clamped - weight_spread.astype(f32) * mean_value
    mean_low = weight_mean.astype(bf16)
    weights = jnp.concatenate(
        [
            mean_low,
            weight_spread,
            (agg_grad[:, 1] / up_total).astype(bf16),
            (agg_grad[:, 2] / down_total).astype(bf16),
            (weight_mean - mean_low.astype(f32)).astype(bf16),
        ],
        1,
    )
    weights = jnp.pad(weights, ((0, WIN), (0, 0)))
    early = lax.psum((w_lin_grad, w_post_x_grad, w_post_agg_grad), both)
    dst_sum, src_sum, feat_sum = backward_edges(order, messages, feat, weights, table.shape[0])
    b_pre_grad = jnp.sum(dst_sum, 0)
    dst_grad = dst_sum[:nodes].astype(bf16)
    src_grad = src_sum.astype(bf16)
    high = lax.Precision.HIGHEST
    w_edg_grad = jnp.dot(w_edge.T.astype(f32), feat_sum, precision=high)
    w_edge_grad = jnp.dot(feat_sum, w_edg.T.astype(f32), precision=high)
    w_dst_grad = dot_tn(node_feat, dst_grad)
    w_src_grad = dot_tn(table, src_grad)
    input_grad = input_grad + dot_nt(dst_grad, w_dst) + dot_nt(src_grad[:nodes], w_src)
    back = nodes + pair_size
    pair_return = from_partner(src_grad[nodes:back], "grp", 0)
    upper_return = passed_along(src_grad[back : back + side_size], "region", -1)
    lower_return = passed_along(src_grad[back + side_size :], "region", 1)
    returned = jnp.concatenate([pair_return, lower_return, upper_return], 0)
    place = (send_rows[None, :] == jnp.arange(nodes)[:, None]).astype(bf16)
    returned = dot(place, dot_nt(returned, w_src).astype(bf16))
    input_grad = input_grad + returned
    w_pre_grad = jnp.concatenate([w_dst_grad, w_src_grad, w_edg_grad], 0)
    late = lax.psum((w_edge_grad, w_pre_grad, b_pre_grad), both)
    return (
        output,
        input_grad,
        late[0],
        late[1],
        late[2],
        early[1],
        early[2],
        early[0],
        gain_grad,
        bias_grad,
    )


def solution(mesh):
    rows, lanes, flat_spec = P(("region", "grp"), None), P(None, ("region", "grp")), P(("region", "grp"))
    return jax.shard_map(
        per_device,
        mesh=mesh,
        in_specs=(rows, lanes) + (flat_spec,) * 5 + (P(),) * 8 + (rows,),
        out_specs=(rows, rows) + (P(),) * 8,
        check_vma=False,
    )
```

```python
import functools
import jax
import jax.numpy as jnp
from jax import lax
from jax.experimental import pallas as pl
from jax.experimental.pallas import tpu as pltpu
from jax.sharding import PartitionSpec as P

TOWERS = 4
SUB = 512
WIN = 128
LANES = 128
ROWS_EL = 1024
bf16 = jnp.bfloat16
f32 = jnp.float32
i32 = jnp.int32
VMEM = pl.BlockSpec(memory_space=pltpu.VMEM)
SMEM = pl.BlockSpec(memory_space=pltpu.SMEM)


def params(**kw):
    return pltpu.CompilerParams(vmem_limit_bytes=60 * 2**20, **kw)


def dot(a, b):
    return jnp.dot(a, b, preferred_element_type=f32)


def dot_nt(a, b):
    return lax.dot_general(a, b, (((1,), (1,)), ((), ())), preferred_element_type=f32)


def dot_tn(a, b):
    return lax.dot_general(a, b, (((0,), (0,)), ((), ())), preferred_element_type=f32)


def bitonic(key, pay):
    n = LANES
    regs = key.shape[0] // 8
    sub_bits, reg_bits = 3, regs.bit_length() - 1
    low_bits = sub_bits + reg_bits
    total = low_bits + 7
    keys = [key[8 * v : 8 * v + 8] for v in range(regs)]
    pays = [pay[8 * v : 8 * v + 8] for v in range(regs)]
    sub = lax.broadcasted_iota(i32, (8, n), 0)
    lane = lax.broadcasted_iota(i32, (8, n), 1)

    def bit_of(b, v):
        if b < sub_bits:
            return ((sub >> b) & 1) == 1
        if b < low_bits:
            return bool((v >> (b - sub_bits)) & 1)
        if b < total:
            return ((lane >> (b - low_bits)) & 1) == 1
        return False

    def flip(mask, by):
        if isinstance(by, bool):
            return jnp.logical_not(mask) if by else mask
        return jnp.logical_xor(mask, by)

    for k in range(total):
        for j in range(k, -1, -1):
            if sub_bits <= j < low_bits:
                d = 1 << (j - sub_bits)
                for v in range(regs):
                    if v & d:
                        continue
                    w = v | d
                    a, b, pa, pb = keys[v], keys[w], pays[v], pays[w]
                    swap = flip(a > b, bit_of(k + 1, v))
                    keys[v], keys[w] = jnp.where(swap, b, a), jnp.where(swap, a, b)
                    pays[v], pays[w] = jnp.where(swap, pb, pa), jnp.where(swap, pa, pb)
                continue
            if j < sub_bits:
                d, axis, size = 1 << j, 0, 8
            else:
                d, axis, size = 1 << (j - low_bits), 1, n
            bit = bit_of(j, 0)

            def partner(x):
                up = pltpu.roll(x, d, axis)
                if 2 * d == size:
                    return up
                return jnp.where(bit, up, pltpu.roll(x, size - d, axis))

            for v in range(regs):
                a, pa = keys[v], pays[v]
                b, pb = partner(a), partner(pa)
                take = jnp.logical_xor(a > b, flip(bit, bit_of(k + 1, v)))
                keys[v], pays[v] = jnp.where(take, b, a), jnp.where(take, pb, pa)
    return jnp.concatenate(keys, 0), jnp.concatenate(pays, 0)


def sort_kernel(nodes, count, dst, src, perm_col, dst_col, dst_row, dst_idx, src_idx):
    rows = dst.shape[0]
    place = lax.broadcasted_iota(i32, (rows, LANES), 0) * LANES + lax.broadcasted_iota(
        i32, (rows, LANES), 1
    )
    total = rows * LANES
    shift = total.bit_length() - 1
    target = jnp.where(place < count[0], dst[...], nodes)
    key, pay = bitonic((target << shift) | place, src[...])
    perm_col[...] = key & (total - 1)
    target = key >> shift
    dst_col[...] = target
    row = target.T
    dst_row[...] = row
    dst_idx[...] = 2 * jnp.minimum(row, nodes - 1)
    src_idx[...] = 2 * pay.T


def sort_edges(edge_dst, edge_src, edge_count, nodes):
    rows = edge_dst.shape[0] // LANES
    shape = jax.ShapeDtypeStruct((rows, LANES), i32)
    return pl.pallas_call(
        functools.partial(sort_kernel, nodes),
        out_shape=[shape] * 5,
        in_specs=[SMEM, VMEM, VMEM],
        out_specs=[VMEM] * 5,
        compiler_params=params(),
        name="sort_edges",
    )(edge_count, edge_dst.reshape(rows, LANES), edge_src.reshape(rows, LANES))


def flat(ref):
    n, s, l = ref.shape
    return ref.reshape(n * s, l)


def put_rows(ref, start, value):
    n = value.shape[0]
    for j in range(2):
        flat(ref)[pl.ds(2 * start + j, n, stride=2), :] = value[:, j * LANES : (j + 1) * LANES]


def get_rows(ref, n):
    return jnp.concatenate([flat(ref)[pl.ds(j, n, stride=2), :] for j in range(2)], 1)


def columns_of(col_ref, first):
    turned = pltpu.roll(col_ref[...], (LANES - first) & (LANES - 1), 1)
    return [turned[:, c : c + 1] for c in range(SUB // LANES)]


def i16(x):
    return x.astype(jnp.int16)


ONE = 1.0


def onehot(match):
    return jnp.where(match, jnp.array(1, bf16), jnp.array(0, bf16))


def window_of(dst_idx, row):
    first = dst_idx[row, 0] >> 1
    last = dst_idx[row + SUB // LANES - 1, LANES - 1] >> 1
    base = (first >> 4) << 4
    return base, ((last - base) >> (WIN.bit_length() - 1)) + 1


def target_rows(dst_row, block, base):
    iota = lax.broadcasted_iota(jnp.int16, (WIN, LANES), 0)
    parts = []
    for c in range(SUB // LANES):
        rel = i16(jnp.broadcast_to(dst_row[block, c : c + 1, :] - base, (WIN, LANES)))
        parts.append(onehot(rel == iota))
    return parts


def forward_kernel(
    src_idx,
    dst_idx,
    edge_live,
    table,
    spread_feat,
    perm_col,
    dst_row,
    w_pre,
    w_edge_rep,
    b_pre,
    m_out,
    feat_out,
    acc,
    deg,
    src_part,
    dst_part,
    rows_a,
    rows_b,
    pick,
    vals,
):
    step = pl.program_id(0)
    steps = pl.num_programs(0)
    per_step = m_out.shape[0]
    subs = per_step // SUB
    lines = SUB // LANES
    hidden = w_pre.shape[1]
    nodes = dst_part.shape[0]
    bufs = [rows_a, rows_b]

    def gather(block, into):
        for j in range(SUB):
            r, c = block * lines + j // LANES, j % LANES
            flat(into)[pl.ds(2 * j, 2), :] = (
                flat(src_part)[pl.ds(src_idx[r, c], 2), :]
                + flat(dst_part)[pl.ds(dst_idx[r, c], 2), :]
            )

    @pl.when(step == 0)
    def _():
        acc[...] = jnp.zeros_like(acc)
        deg[...] = jnp.zeros_like(deg)

        @pl.loop(0, table.shape[0] // 256)
        def _(c):
            at = pl.multiple_of(c * 256, 256)
            put_rows(src_part, at, dot(table[pl.ds(at, 256), :], w_pre[hidden : 2 * hidden, :]))

        @pl.loop(0, nodes // 256)
        def _(c):
            at = pl.multiple_of(c * 256, 256)
            put_rows(dst_part, at, dot(table[pl.ds(at, 256), :], w_pre[:hidden, :]))

        gather(0, rows_a)

    def add_window(base, at):
        hot = target_rows(dst_row, at, base)
        total = hot[0].astype(f32)
        for h in hot[1:]:
            total = total + h.astype(f32)
        here = pl.ds(pl.multiple_of(base, 8), WIN)
        deg[here, :] += total
        hot = jnp.concatenate(hot, 1)
        acc[here, :hidden] += dot(hot, vals[:, :hidden])
        acc[here, hidden : 2 * hidden] += dot(hot, vals[:, hidden : 2 * hidden]) + dot(
            hot, vals[:, 2 * hidden : 3 * hidden]
        )
        acc[here, 2 * hidden :] += dot(hot, vals[:, 3 * hidden :])

    for s in range(subs):
        block = step * subs + s
        following = jnp.where(block + 1 < steps * subs, block + 1, 0)
        gather(following, bufs[(s + 1) % 2])
        wide = lax.broadcasted_iota(jnp.int16, (LANES, LANES), 1)
        highs = []
        for c, place in enumerate(columns_of(perm_col, block * lines)):
            low = i16(jnp.broadcast_to(place & (ROWS_EL - 1), (LANES, LANES)))
            highs.append(jnp.broadcast_to(place >> (ROWS_EL.bit_length() - 1), (LANES, hidden)))
            for t in range(ROWS_EL // LANES):
                pick[c * LANES : (c + 1) * LANES, t * LANES : (t + 1) * LANES] = onehot(
                    low == wide + jnp.int16(t * LANES)
                )
        found = dot(pick[...], spread_feat[...])
        high = jnp.concatenate(highs, 0)
        lane = lax.broadcasted_iota(i32, (SUB, hidden), 1)
        found = jnp.where((lane & 15) == high, found, 0.0).astype(bf16)
        select = lax.broadcasted_iota(i32, (16, hidden), 1) >> 4
        select = onehot(select == lax.broadcasted_iota(i32, (16, hidden), 0))
        feat_out[:, s * SUB : (s + 1) * SUB] = dot_nt(select, found).astype(bf16)
        embed = dot(found, w_edge_rep[...]).astype(bf16)
        m = get_rows(bufs[s % 2], SUB) + dot(embed, w_pre[2 * hidden :, :]) + b_pre[...]
        spot = lax.broadcasted_iota(i32, (SUB, hidden), 0) + block * SUB
        m = jnp.where(spot < edge_live[0], m, 0.0)
        m_out[s * SUB : (s + 1) * SUB, :] = m
        low = m.astype(bf16)
        vals[:, :hidden] = low
        wide_low = low.astype(f32)
        square = wide_low * wide_low
        top = square.astype(bf16)
        vals[:, hidden : 2 * hidden] = top
        vals[:, 2 * hidden : 3 * hidden] = (square - top.astype(f32)).astype(bf16)
        vals[:, 3 * hidden : 4 * hidden] = jnp.exp(m).astype(bf16)
        vals[:, 4 * hidden :] = jnp.exp(-m).astype(bf16)
        base, windows = window_of(dst_idx, block * lines)
        add_window(base, block)

        @pl.loop(1, windows)
        def _(w):
            add_window(base + w * WIN, block)


def forward_edges(sorted_edges, edge_count, table, edge_feat, w_edge, w_pre, b_pre, nodes):
    perm_col, dst_col, dst_row, dst_idx, src_idx = sorted_edges
    edges = edge_feat.shape[1]
    hidden = w_pre.shape[1]
    ext = table.shape[0]
    spread_feat = edge_feat.reshape(-1, ROWS_EL).T
    w_edge_rep = jnp.repeat(w_edge, edges // ROWS_EL, axis=0)
    step_edges = 1024
    steps = edges // step_edges
    whole = lambda *shape: pl.BlockSpec(shape, lambda i: (0,) * len(shape))
    return pl.pallas_call(
        forward_kernel,
        grid=(steps,),
        out_shape=[
            jax.ShapeDtypeStruct((edges, hidden), f32),
            jax.ShapeDtypeStruct((16, edges), bf16),
            jax.ShapeDtypeStruct((nodes + WIN, 4 * hidden), f32),
            jax.ShapeDtypeStruct((nodes + WIN, LANES), f32),
        ],
        in_specs=[
            SMEM,
            SMEM,
            SMEM,
            whole(ext, hidden),
            whole(ROWS_EL, hidden),
            whole(LANES, LANES),
            whole(edges // SUB, SUB // LANES, LANES),
            whole(3 * hidden, hidden),
            whole(hidden, hidden),
            whole(1, hidden),
        ],
        out_specs=[
            pl.BlockSpec((step_edges, hidden), lambda i: (i, 0)),
            pl.BlockSpec((16, step_edges), lambda i: (0, i)),
            whole(nodes + WIN, 4 * hidden),
            whole(nodes + WIN, LANES),
        ],
        scratch_shapes=[
            pltpu.VMEM((ext, 2, LANES), f32),
            pltpu.VMEM((nodes, 2, LANES), f32),
            pltpu.VMEM((SUB, 2, LANES), f32),
            pltpu.VMEM((SUB, 2, LANES), f32),
            pltpu.VMEM((SUB, ROWS_EL), bf16),
            pltpu.VMEM((SUB, 5 * hidden), bf16),
        ],
        compiler_params=params(),
        name="forward_edges",
    )(
        src_idx,
        dst_idx,
        edge_count,
        table,
        spread_feat,
        perm_col,
        dst_row.reshape(edges // SUB, SUB // LANES, LANES),
        w_pre,
        w_edge_rep,
        b_pre.reshape(1, hidden),
    )


CHAINS = 4


def backward_kernel(
    src_idx,
    dst_idx,
    m_in,
    feat,
    dst_col,
    dst_row,
    weights,
    dst_sum,
    src_sum,
    feat_sum,
    acc0,
    acc1,
    acc2,
    acc3,
    rows_a,
    rows_b,
    got,
    low,
):
    step = pl.program_id(0)
    steps = pl.num_programs(0)
    subs = m_in.shape[0] // SUB
    lines = SUB // LANES
    hidden = m_in.shape[1]
    accs = [acc0, acc1, acc2, acc3]
    bufs = [rows_a, rows_b]

    @pl.when(step == 0)
    def _():
        for ref in accs + bufs:
            ref[...] = jnp.zeros_like(ref)
        dst_sum[...] = jnp.zeros_like(dst_sum)
        feat_sum[...] = jnp.zeros_like(feat_sum)

    def scatter(block, rows):
        for j in range(SUB):
            into = flat(accs[j % CHAINS])
            at = pl.ds(src_idx[block * lines + j // LANES, j % LANES], 2)
            into[at, :] = into[at, :] + flat(rows)[pl.ds(2 * j, 2), :]

    def take_window(block, base, more):
        wide = lax.broadcasted_iota(jnp.int16, (LANES, WIN), 1)
        hot = []
        for place in columns_of(dst_col, block * lines):
            hot.append(onehot(i16(jnp.broadcast_to(place - base, (LANES, WIN))) == wide))
        hot = jnp.concatenate(hot, 0)
        here = pl.ds(pl.multiple_of(base, 16), WIN)
        for q in range(4):
            part = dot(hot, weights[here, q * hidden : (q + 1) * hidden])
            if q == 0:
                part = part + dot(hot, weights[here, 4 * hidden :])
            to = slice(q * hidden, (q + 1) * hidden)
            got[:, to] = got[:, to] + part if more else part

    def add_window(block, base):
        hot = jnp.concatenate(target_rows(dst_row, block, base), 1)
        dst_sum[pl.ds(pl.multiple_of(base, 8), WIN), :] += dot(hot, low[...])

    for s in range(subs):
        block = step * subs + s
        scatter(jnp.maximum(block - 1, 0), bufs[(s + 1) % 2])
        base, windows = window_of(dst_idx, block * lines)
        take_window(block, base, False)

        @pl.loop(1, windows)
        def _(w):
            take_window(block, base + w * WIN, True)

        m = m_in[s * SUB : (s + 1) * SUB, :]
        grad = (
            got[:, :hidden]
            + got[:, hidden : 2 * hidden] * m.astype(bf16).astype(f32)
            + got[:, 2 * hidden : 3 * hidden] * jnp.exp(m).astype(bf16).astype(f32)
            + got[:, 3 * hidden : 4 * hidden] * jnp.exp(-m).astype(bf16).astype(f32)
        ).astype(bf16)
        low[...] = grad
        put_rows(bufs[s % 2], 0, grad.astype(f32))
        feat_sum[...] += dot(feat[:, s * SUB : (s + 1) * SUB], low[...])
        add_window(block, base)

        @pl.loop(1, windows)
        def _(w):
            add_window(block, base + w * WIN)

    @pl.when(step == steps - 1)
    def _():
        scatter(steps * subs - 1, bufs[(subs - 1) % 2])

        @pl.loop(0, src_sum.shape[0] // 256)
        def _(c):
            at = pl.multiple_of(c * 256, 256)
            for j in range(2):
                here = pl.ds(2 * at + j, 256, stride=2)
                src_sum[pl.ds(at, 256), j * LANES : (j + 1) * LANES] = (
                    flat(acc0)[here, :] + flat(acc1)[here, :]
                ) + (flat(acc2)[here, :] + flat(acc3)[here, :])


def backward_edges(sorted_edges, messages, feat, weights, ext):
    perm_col, dst_col, dst_row, dst_idx, src_idx = sorted_edges
    edges, hidden = messages.shape
    padded = weights.shape[0]
    step_edges = 2 * SUB
    whole = lambda *shape: pl.BlockSpec(shape, lambda i: (0,) * len(shape))
    return pl.pallas_call(
        backward_kernel,
        grid=(edges // step_edges,),
        out_shape=[
            jax.ShapeDtypeStruct((padded, hidden), f32),
            jax.ShapeDtypeStruct((ext, hidden), f32),
            jax.ShapeDtypeStruct((16, hidden), f32),
        ],
        in_specs=[
            SMEM,
            SMEM,
            pl.BlockSpec((step_edges, hidden), lambda i: (i, 0)),
            pl.BlockSpec((16, step_edges), lambda i: (0, i)),
            whole(LANES, LANES),
            whole(edges // SUB, SUB // LANES, LANES),
            whole(padded, 5 * hidden),
        ],
        out_specs=[whole(padded, hidden), whole(ext, hidden), whole(16, hidden)],
        scratch_shapes=[pltpu.VMEM((ext, 2, LANES), f32)] * CHAINS
        + [pltpu.VMEM((SUB, 2, LANES), f32)] * 2
        + [pltpu.VMEM((SUB, 4 * hidden), f32), pltpu.VMEM((SUB, hidden), bf16)],
        compiler_params=params(),
        name="backward_edges",
    )(
        src_idx,
        dst_idx,
        messages,
        feat,
        dst_col,
        dst_row.reshape(edges // SUB, SUB // LANES, LANES),
        weights,
    )


MESH = pl.DeviceIdType.MESH


def low_count(regions):
    bits = regions.bit_length() - 1
    return 1 << ((bits + 1) // 2)


def all_sum_kernel(n_low, n_high, x, out, buf1, buf2, send1, recv1, send2, recv2):
    region, grp = lax.axis_index("region"), lax.axis_index("grp")
    low, high = lax.rem(region, n_low), region // n_low
    n1 = 2 * n_low
    me1, me2 = low * 2 + grp, high

    def peer1(k):
        p = lax.rem(me1 + k, n1)
        return p, (high * n_low + p // 2, lax.rem(p, 2))

    def peer2(k):
        p = lax.rem(me2 + k, n_high)
        return p, (p * n_low + low, grp)

    barrier = pltpu.get_barrier_semaphore()
    for k in range(1, n1):
        pl.semaphore_signal(barrier, inc=1, device_id=peer1(k)[1], device_id_type=MESH)
    for k in range(1, n_high):
        pl.semaphore_signal(barrier, inc=1, device_id=peer2(k)[1], device_id_type=MESH)
    pl.semaphore_wait(barrier, n1 + n_high - 2)

    def stage(count, me, peer, buf, send, recv):
        copies = []
        for k in range(1, count):
            copy = pltpu.make_async_remote_copy(
                src_ref=buf.at[me],
                dst_ref=buf.at[me],
                send_sem=send.at[k],
                recv_sem=recv.at[me],
                device_id=peer(k)[1],
                device_id_type=MESH,
            )
            copy.start()
            copies.append(copy)
        for k in range(1, count):
            p, where = peer(k)
            pltpu.make_async_remote_copy(
                src_ref=buf.at[p],
                dst_ref=buf.at[p],
                send_sem=send.at[k],
                recv_sem=recv.at[p],
                device_id=where,
                device_id_type=MESH,
            ).wait_recv()
        for copy in copies:
            copy.wait_send()
        total = buf[0]
        for i in range(1, count):
            total = total + buf[i]
        return total

    buf1[me1] = x[...]
    buf2[me2] = stage(n1, me1, peer1, buf1, send1, recv1)
    out[...] = stage(n_high, me2, peer2, buf2, send2, recv2)


def all_sum(x, collective_id):
    regions = lax.axis_size("region")
    n_low = low_count(regions)
    n_high = regions // n_low
    dma = pltpu.SemaphoreType.DMA
    return pl.pallas_call(
        functools.partial(all_sum_kernel, n_low, n_high),
        out_shape=jax.ShapeDtypeStruct(x.shape, x.dtype),
        in_specs=[VMEM],
        out_specs=VMEM,
        scratch_shapes=[
            pltpu.VMEM((2 * n_low,) + x.shape, x.dtype),
            pltpu.VMEM((n_high,) + x.shape, x.dtype),
            dma((2 * n_low,)),
            dma((2 * n_low,)),
            dma((n_high,)),
            dma((n_high,)),
        ],
        compiler_params=pltpu.CompilerParams(
            collective_id=collective_id, has_side_effects=True
        ),
        name="all_sum_%d" % collective_id,
    )(x)


avg_log_degree = 2.2
norm_eps = 1e-05
CHUNK = 256


def live_mask(node_live, step, width):
    spot = lax.broadcasted_iota(i32, (CHUNK, width), 0) + step * CHUNK
    return jnp.where(spot < node_live[0], 1.0, 0.0)


def aggregates(acc, deg):
    hidden = acc.shape[1] // 4
    degree = jnp.sum(deg[...], 1, keepdims=True)
    clamped = jnp.maximum(degree, 1.0)
    log_count = jnp.log(degree + 1.0)
    amplify = log_count / avg_log_degree
    attenuate = avg_log_degree / jnp.log(clamped + 1.0)
    share = 1.0 / clamped
    mean = acc[:, :hidden] / clamped
    square = acc[:, hidden : 2 * hidden] / clamped
    spread = jnp.sqrt(jnp.maximum(square - mean * mean, 0.0) + 1.0)
    up = acc[:, 2 * hidden : 3 * hidden] + 1.0
    down = acc[:, 3 * hidden :] + 1.0
    soft_max = jnp.log(up) - log_count
    soft_min = log_count - jnp.log(down)
    return (mean, soft_max, soft_min, spread), (None, amplify, attenuate), share, up, down


def scaled(value, scale):
    return (value if scale is None else value * scale).astype(bf16)


def spread_towers(w_post_agg, towers_w):
    hidden = w_post_agg.shape[1]
    width = hidden // TOWERS
    row = lax.broadcasted_iota(i32, (hidden, hidden), 0) // width
    col = lax.broadcasted_iota(i32, (hidden, hidden), 1) // width
    for k in range(12):
        part = w_post_agg[k * width : (k + 1) * width, :]
        tall = jnp.concatenate([part] * TOWERS, 0).astype(f32)
        towers_w[k] = jnp.where(row == col, tall, 0.0).astype(bf16)


def node_forward_kernel(
    node_live, acc, deg, node_feat, w_post_x, w_post_agg, w_lin, post, lin, stats, towers_w
):
    step = pl.program_id(0)

    @pl.when(step == 0)
    def _():
        spread_towers(w_post_agg, towers_w)
        stats[...] = jnp.zeros_like(stats)

    parts, scales, _, _, _ = aggregates(acc, deg)
    total = dot(node_feat[...], w_post_x[...])
    for s in range(3):
        for a in range(4):
            total = total + dot(scaled(parts[a], scales[s]), towers_w[4 * s + a])
    post[...] = total.astype(bf16)
    out = dot(post[...], w_lin[...])
    lin[...] = out
    mask = live_mask(node_live, step, out.shape[1])
    masked = out * mask
    stats[0:1, :] += jnp.sum(masked, 0, keepdims=True)
    stats[1:2, :] += jnp.sum(masked * out, 0, keepdims=True)
    stats[2:3, :] += jnp.sum(mask, 0, keepdims=True)


def whole_spec(*shape):
    return pl.BlockSpec(shape, lambda i: (0,) * len(shape))


def chunk_spec(width, rows=CHUNK):
    return pl.BlockSpec((rows, width), lambda i: (i, 0))


def node_forward(node_count, acc, deg, node_feat, w_post_x, w_post_agg, w_lin):
    nodes, hidden = node_feat.shape
    return pl.pallas_call(
        node_forward_kernel,
        grid=(nodes // CHUNK,),
        out_shape=[
            jax.ShapeDtypeStruct((nodes, hidden), bf16),
            jax.ShapeDtypeStruct((nodes, hidden), f32),
            jax.ShapeDtypeStruct((8, hidden), f32),
        ],
        in_specs=[
            SMEM,
            chunk_spec(4 * hidden),
            chunk_spec(LANES),
            chunk_spec(hidden),
            whole_spec(hidden, hidden),
            whole_spec(3 * hidden, hidden),
            whole_spec(hidden, hidden),
        ],
        out_specs=[chunk_spec(hidden), chunk_spec(hidden), whole_spec(8, hidden)],
        scratch_shapes=[pltpu.VMEM((12, hidden, hidden), bf16)],
        compiler_params=params(),
        name="node_forward",
    )(node_count, acc, deg, node_feat, w_post_x, w_post_agg, w_lin)


SLOPE = 0.7978845608028654
CUBE = 0.044715


def norm_of(stats, lin, norm):
    count = stats[2:3, :]
    centre = stats[0:1, :] / count
    inverse = lax.rsqrt(stats[1:2, :] / count - centre * centre + norm_eps)
    normed = (lin[...] - centre) * inverse
    return normed, normed * norm[0:1, :] + norm[1:2, :], inverse, count


def gelu_parts(v):
    half = 0.5 * (1.0 + jnp.tanh(SLOPE * (v + CUBE * v * v * v)))
    slope = half + v * 2.0 * half * (1.0 - half) * SLOPE * (1.0 + 3.0 * CUBE * v * v)
    return v * half, slope


def node_middle_kernel(node_live, stats, norm, lin, node_feat, out_grad, output, sums):
    step = pl.program_id(0)

    @pl.when(step == 0)
    def _():
        sums[...] = jnp.zeros_like(sums)

    normed, shifted, _, _ = norm_of(stats, lin, norm)
    mask = live_mask(node_live, step, lin.shape[1])
    value, slope = gelu_parts(shifted)
    output[...] = (node_feat[...].astype(f32) + mask * value).astype(bf16)
    grad = out_grad[...].astype(f32) * mask * slope
    sums[0:1, :] += jnp.sum(grad, 0, keepdims=True)
    sums[1:2, :] += jnp.sum(grad * normed, 0, keepdims=True)


def node_middle(node_count, stats, norm, lin, node_feat, out_grad):
    nodes, hidden = node_feat.shape
    return pl.pallas_call(
        node_middle_kernel,
        grid=(nodes // CHUNK,),
        out_shape=[
            jax.ShapeDtypeStruct((nodes, hidden), bf16),
            jax.ShapeDtypeStruct((8, hidden), f32),
        ],
        in_specs=[SMEM, whole_spec(8, hidden), whole_spec(2, hidden)] + [chunk_spec(hidden)] * 3,
        out_specs=[chunk_spec(hidden), whole_spec(8, hidden)],
        compiler_params=params(),
        name="node_middle",
    )(node_count, stats, norm, lin, node_feat, out_grad)


def node_backward_kernel(
    node_live,
    stats,
    sums,
    norm,
    acc,
    deg,
    lin,
    post,
    node_feat,
    out_grad,
    w_post_x,
    w_post_agg,
    w_lin,
    weights,
    input_grad,
    w_lin_grad,
    w_post_x_grad,
    w_agg_grad,
    towers_w,
    agg_sum,
):
    step = pl.program_id(0)
    hidden = lin.shape[1]

    @pl.when(step == 0)
    def _():
        spread_towers(w_post_agg, towers_w)
        weights[pl.ds(lin.shape[0] * pl.num_programs(0), WIN), :] = jnp.zeros((WIN, 5 * hidden), bf16)
        w_lin_grad[...] = jnp.zeros_like(w_lin_grad)
        w_post_x_grad[...] = jnp.zeros_like(w_post_x_grad)
        agg_sum[...] = jnp.zeros_like(agg_sum)

    normed, shifted, inverse, count = norm_of(stats, lin, norm)
    mask = live_mask(node_live, step, hidden)
    upstream = out_grad[...].astype(f32)
    shift_grad = upstream * mask * gelu_parts(shifted)[1]
    lin_grad = (
        mask
        * inverse
        * norm[0:1, :]
        * (shift_grad - sums[0:1, :] / count - normed * (sums[1:2, :] / count))
    ).astype(bf16)
    post_grad = dot_nt(lin_grad, w_lin[...]).astype(bf16)
    w_lin_grad[...] += dot_tn(post[...], lin_grad)
    w_post_x_grad[...] += dot_tn(node_feat[...], post_grad)
    input_grad[...] = upstream + dot_nt(post_grad, w_post_x[...])
    parts, scales, share, up, down = aggregates(acc, deg)
    turned = post_grad.T
    grads = []
    for a in range(4):
        grad = None
        for s in range(3):
            k = 4 * s + a
            agg_sum[k] += dot(turned, scaled(parts[a], scales[s]))
            piece = dot_nt(post_grad, towers_w[k])
            piece = piece if s == 0 else piece * scales[s]
            grad = piece if grad is None else grad + piece
        grads.append(grad)
    mean, _, _, spread = parts
    ws = (grads[3] / spread * share).astype(bf16)
    wu, wd = grads[1] / up, grads[2] / down
    wu_low, wd_low = wu.astype(bf16), wd.astype(bf16)
    wm = grads[0] - ws.astype(f32) * mean / share
    wm = wm + (wu - wu_low.astype(f32)) * (up - 1.0) + (wd - wd_low.astype(f32)) * (down - 1.0)
    wm = wm * share
    wm_low = wm.astype(bf16)
    here = pl.ds(pl.multiple_of(step * CHUNK, CHUNK), CHUNK)
    wm_rest = (wm - wm_low.astype(f32)).astype(bf16)
    for q, value in enumerate((wm_low, ws, wu_low, wd_low, wm_rest)):
        weights[here, q * hidden : (q + 1) * hidden] = value

    @pl.when(step == pl.num_programs(0) - 1)
    def _():
        width = hidden // TOWERS
        row = lax.broadcasted_iota(i32, (hidden, hidden), 0) // width
        col = lax.broadcasted_iota(i32, (hidden, hidden), 1) // width
        for k in range(12):
            block = jnp.where(row == col, agg_sum[k], 0.0).T
            total = block[:width]
            for t in range(1, TOWERS):
                total = total + block[t * width : (t + 1) * width]
            w_agg_grad[k * width : (k + 1) * width, :] = total


def node_backward(
    node_count, stats, sums, norm, acc, deg, lin, post, node_feat, out_grad, w_post_x, w_post_agg, w_lin
):
    nodes, hidden = node_feat.shape
    return pl.pallas_call(
        node_backward_kernel,
        grid=(nodes // CHUNK,),
        out_shape=[
            jax.ShapeDtypeStruct((nodes + WIN, 5 * hidden), bf16),
            jax.ShapeDtypeStruct((nodes, hidden), f32),
            jax.ShapeDtypeStruct((hidden, hidden), f32),
            jax.ShapeDtypeStruct((hidden, hidden), f32),
            jax.ShapeDtypeStruct((3 * hidden, hidden), f32),
        ],
        in_specs=[
            SMEM,
            whole_spec(8, hidden),
            whole_spec(8, hidden),
            whole_spec(2, hidden),
            chunk_spec(4 * hidden),
            chunk_spec(LANES),
            chunk_spec(hidden),
            chunk_spec(hidden),
            chunk_spec(hidden),
            chunk_spec(hidden),
            whole_spec(hidden, hidden),
            whole_spec(3 * hidden, hidden),
            whole_spec(hidden, hidden),
        ],
        out_specs=[
            whole_spec(nodes + WIN, 5 * hidden),
            chunk_spec(hidden),
            whole_spec(hidden, hidden),
            whole_spec(hidden, hidden),
            whole_spec(3 * hidden, hidden),
        ],
        scratch_shapes=[
            pltpu.VMEM((12, hidden, hidden), bf16),
            pltpu.VMEM((12, hidden, hidden), f32),
        ],
        compiler_params=params(),
        name="node_backward",
    )(
        node_count,
        stats,
        sums,
        norm,
        acc,
        deg,
        lin,
        post,
        node_feat,
        out_grad,
        w_post_x,
        w_post_agg,
        w_lin,
    )


def from_partner(block, axis, stride):
    count = lax.axis_size(axis)
    route = []
    for low in range(count):
        high = low | 1 << stride
        if high != low and high < count:
            route += [(low, high), (high, low)]
    return lax.ppermute(block, axis, route)


def passed_along(value, axis, steps):
    count = lax.axis_size(axis)
    first, last = (max(0, -steps), min(count, count - steps))
    return lax.ppermute(value, axis, [(source, source + steps) for source in range(first, last)])


def per_device(
    node_feat,
    edge_feat,
    edge_src,
    edge_dst,
    send_rows,
    node_count,
    edge_count,
    w_edge,
    w_pre,
    b_pre,
    w_post_x,
    w_post_agg,
    w_lin,
    norm_gain,
    norm_bias,
    out_grad,
):
    nodes, hidden = node_feat.shape
    pair_size, side_size = nodes // 4, nodes // 8
    sent = jnp.take(node_feat, send_rows, axis=0)
    pair_in = from_partner(sent[:pair_size], "grp", 0)
    from_lower = passed_along(sent[pair_size + side_size :], "region", 1)
    from_upper = passed_along(sent[pair_size : pair_size + side_size], "region", -1)
    table = jnp.concatenate([node_feat, pair_in, from_lower, from_upper], 0)
    w_dst, w_src, w_edg = w_pre[:hidden], w_pre[hidden : 2 * hidden], w_pre[2 * hidden :]

    order = sort_edges(edge_dst, edge_src, edge_count, nodes)
    messages, feat, acc, deg = forward_edges(
        order, edge_count, table, edge_feat, w_edge, w_pre, b_pre, nodes
    )
    post, lin, stats = node_forward(
        node_count, acc, deg, node_feat, w_post_x, w_post_agg, w_lin
    )
    stats = all_sum(stats, 0)
    norm = jnp.stack([norm_gain, norm_bias])
    output, sums = node_middle(node_count, stats, norm, lin, node_feat, out_grad)
    sums = all_sum(sums, 1)
    weights, input_grad, w_lin_grad, w_post_x_grad, w_post_agg_grad = node_backward(
        node_count, stats, sums, norm, acc, deg, lin, post, node_feat, out_grad,
        w_post_x, w_post_agg, w_lin,
    )
    both = ("region", "grp")
    early = lax.psum((w_lin_grad, w_post_x_grad, w_post_agg_grad), both)
    dst_sum, src_sum, feat_sum = backward_edges(order, messages, feat, weights, table.shape[0])
    b_pre_grad = jnp.sum(dst_sum, 0)
    dst_grad = dst_sum[:nodes].astype(bf16)
    src_grad = src_sum.astype(bf16)
    high = lax.Precision.HIGHEST
    w_edg_grad = jnp.dot(w_edge.T.astype(f32), feat_sum, precision=high)
    w_edge_grad = jnp.dot(feat_sum, w_edg.T.astype(f32), precision=high)
    w_dst_grad = dot_tn(node_feat, dst_grad)
    w_src_grad = dot_tn(table, src_grad)
    input_grad = input_grad + dot_nt(dst_grad, w_dst) + dot_nt(src_grad[:nodes], w_src)
    back = nodes + pair_size
    pair_return = from_partner(src_grad[nodes:back], "grp", 0)
    upper_return = passed_along(src_grad[back : back + side_size], "region", -1)
    lower_return = passed_along(src_grad[back + side_size :], "region", 1)
    returned = jnp.concatenate([pair_return, lower_return, upper_return], 0)
    place = (send_rows[None, :] == jnp.arange(nodes)[:, None]).astype(bf16)
    returned = dot(place, returned)
    top = returned.astype(bf16)
    rest = (returned - top.astype(f32)).astype(bf16)
    input_grad = input_grad + dot_nt(top, w_src) + dot_nt(rest, w_src)
    w_pre_grad = jnp.concatenate([w_dst_grad, w_src_grad, w_edg_grad], 0)
    late = lax.psum((w_edge_grad, w_pre_grad, b_pre_grad), both)
    return (
        output,
        input_grad,
        late[0],
        late[1],
        late[2],
        early[1],
        early[2],
        early[0],
        sums[1],
        sums[0],
    )


def solution(mesh):
    rows, lanes, flat_spec = P(("region", "grp"), None), P(None, ("region", "grp")), P(("region", "grp"))
    return jax.shard_map(
        per_device,
        mesh=mesh,
        in_specs=(rows, lanes) + (flat_spec,) * 5 + (P(),) * 8 + (rows,),
        out_specs=(rows, rows) + (P(),) * 8,
        check_vma=False,
    )
```

```python
import functools
import jax
import jax.numpy as jnp
from jax import lax
from jax.experimental import pallas as pl
from jax.experimental.pallas import tpu as pltpu
from jax.sharding import PartitionSpec as P

TOWERS = 4
SUB = 512
WIN = 128
LANES = 128
ROWS_EL = 1024
bf16 = jnp.bfloat16
f32 = jnp.float32
i32 = jnp.int32
VMEM = pl.BlockSpec(memory_space=pltpu.VMEM)
SMEM = pl.BlockSpec(memory_space=pltpu.SMEM)


def params(**kw):
    return pltpu.CompilerParams(vmem_limit_bytes=60 * 2**20, **kw)


def dot(a, b):
    return jnp.dot(a, b, preferred_element_type=f32)


def dot_nt(a, b):
    return lax.dot_general(a, b, (((1,), (1,)), ((), ())), preferred_element_type=f32)


def dot_tn(a, b):
    return lax.dot_general(a, b, (((0,), (0,)), ((), ())), preferred_element_type=f32)


def bitonic(key, pay):
    n = LANES
    regs = key.shape[0] // 8
    sub_bits, reg_bits = 3, regs.bit_length() - 1
    low_bits = sub_bits + reg_bits
    total = low_bits + 7
    keys = [key[8 * v : 8 * v + 8] for v in range(regs)]
    pays = [pay[8 * v : 8 * v + 8] for v in range(regs)]
    sub = lax.broadcasted_iota(i32, (8, n), 0)
    lane = lax.broadcasted_iota(i32, (8, n), 1)

    def bit_of(b, v):
        if b < sub_bits:
            return ((sub >> b) & 1) == 1
        if b < low_bits:
            return bool((v >> (b - sub_bits)) & 1)
        if b < total:
            return ((lane >> (b - low_bits)) & 1) == 1
        return False

    def flip(mask, by):
        if isinstance(by, bool):
            return jnp.logical_not(mask) if by else mask
        return jnp.logical_xor(mask, by)

    for k in range(total):
        for j in range(k, -1, -1):
            if sub_bits <= j < low_bits:
                d = 1 << (j - sub_bits)
                for v in range(regs):
                    if v & d:
                        continue
                    w = v | d
                    a, b, pa, pb = keys[v], keys[w], pays[v], pays[w]
                    swap = flip(a > b, bit_of(k + 1, v))
                    keys[v], keys[w] = jnp.where(swap, b, a), jnp.where(swap, a, b)
                    pays[v], pays[w] = jnp.where(swap, pb, pa), jnp.where(swap, pa, pb)
                continue
            if j < sub_bits:
                d, axis, size = 1 << j, 0, 8
            else:
                d, axis, size = 1 << (j - low_bits), 1, n
            bit = bit_of(j, 0)

            def partner(x):
                up = pltpu.roll(x, d, axis)
                if 2 * d == size:
                    return up
                return jnp.where(bit, up, pltpu.roll(x, size - d, axis))

            for v in range(regs):
                a, pa = keys[v], pays[v]
                b, pb = partner(a), partner(pa)
                take = jnp.logical_xor(a > b, flip(bit, bit_of(k + 1, v)))
                keys[v], pays[v] = jnp.where(take, b, a), jnp.where(take, pb, pa)
    return jnp.concatenate(keys, 0), jnp.concatenate(pays, 0)


def sort_kernel(nodes, count, dst, src, perm_col, dst_col, dst_row, dst_idx, src_idx):
    rows = dst.shape[0]
    place = lax.broadcasted_iota(i32, (rows, LANES), 0) * LANES + lax.broadcasted_iota(
        i32, (rows, LANES), 1
    )
    total = rows * LANES
    shift = total.bit_length() - 1
    target = jnp.where(place < count[0], dst[...], nodes)
    key, pay = bitonic((target << shift) | place, src[...])
    perm_col[...] = key & (total - 1)
    target = key >> shift
    dst_col[...] = target
    row = target.T
    dst_row[...] = row
    dst_idx[...] = 2 * jnp.minimum(row, nodes - 1)
    src_idx[...] = 2 * pay.T


def sort_edges(edge_dst, edge_src, edge_count, nodes):
    rows = edge_dst.shape[0] // LANES
    shape = jax.ShapeDtypeStruct((rows, LANES), i32)
    return pl.pallas_call(
        functools.partial(sort_kernel, nodes),
        out_shape=[shape] * 5,
        in_specs=[SMEM, VMEM, VMEM],
        out_specs=[VMEM] * 5,
        compiler_params=params(),
        name="sort_edges",
    )(edge_count, edge_dst.reshape(rows, LANES), edge_src.reshape(rows, LANES))


def flat(ref):
    n, s, l = ref.shape
    return ref.reshape(n * s, l)


def put_rows(ref, start, value):
    n = value.shape[0]
    for j in range(2):
        flat(ref)[pl.ds(2 * start + j, n, stride=2), :] = value[:, j * LANES : (j + 1) * LANES]


def get_rows(ref, n):
    return jnp.concatenate([flat(ref)[pl.ds(j, n, stride=2), :] for j in range(2)], 1)


def columns_of(col_ref, first):
    turned = pltpu.roll(col_ref[...], (LANES - first) & (LANES - 1), 1)
    return [turned[:, c : c + 1] for c in range(SUB // LANES)]


def i16(x):
    return x.astype(jnp.int16)


ONE = 1.0


def onehot(match):
    return jnp.where(match, jnp.array(1, bf16), jnp.array(0, bf16))


def window_of(dst_idx, row):
    first = dst_idx[row, 0] >> 1
    last = dst_idx[row + SUB // LANES - 1, LANES - 1] >> 1
    base = (first >> 4) << 4
    return base, ((last - base) >> (WIN.bit_length() - 1)) + 1


def target_rows(dst_row, block, base):
    iota = lax.broadcasted_iota(jnp.int16, (WIN, LANES), 0)
    parts = []
    for c in range(SUB // LANES):
        rel = i16(jnp.broadcast_to(dst_row[block, c : c + 1, :] - base, (WIN, LANES)))
        parts.append(onehot(rel == iota))
    return parts


def forward_kernel(
    src_idx,
    dst_idx,
    edge_live,
    table,
    spread_feat,
    perm_col,
    dst_row,
    w_pre,
    w_edge_rep,
    b_pre,
    m_out,
    feat_out,
    acc,
    deg,
    src_part,
    dst_part,
    rows_a,
    rows_b,
    pick,
    vals,
):
    step = pl.program_id(0)
    steps = pl.num_programs(0)
    per_step = m_out.shape[0]
    subs = per_step // SUB
    lines = SUB // LANES
    hidden = w_pre.shape[1]
    nodes = dst_part.shape[0]
    bufs = [rows_a, rows_b]

    def gather(block, into):
        for j in range(SUB):
            r, c = block * lines + j // LANES, j % LANES
            flat(into)[pl.ds(2 * j, 2), :] = (
                flat(src_part)[pl.ds(src_idx[r, c], 2), :]
                + flat(dst_part)[pl.ds(dst_idx[r, c], 2), :]
            )

    @pl.when(step == 0)
    def _():
        acc[...] = jnp.zeros_like(acc)
        deg[...] = jnp.zeros_like(deg)

        @pl.loop(0, table.shape[0] // 256)
        def _(c):
            at = pl.multiple_of(c * 256, 256)
            put_rows(src_part, at, dot(table[pl.ds(at, 256), :], w_pre[hidden : 2 * hidden, :]))

        @pl.loop(0, nodes // 256)
        def _(c):
            at = pl.multiple_of(c * 256, 256)
            put_rows(dst_part, at, dot(table[pl.ds(at, 256), :], w_pre[:hidden, :]))

        gather(0, rows_a)

    def add_window(base, at):
        hot = target_rows(dst_row, at, base)
        total = hot[0].astype(f32)
        for h in hot[1:]:
            total = total + h.astype(f32)
        here = pl.ds(pl.multiple_of(base, 8), WIN)
        deg[here, :] += total
        hot = jnp.concatenate(hot, 1)
        acc[here, :hidden] += dot(hot, vals[:, :hidden])
        acc[here, hidden : 2 * hidden] += dot(hot, vals[:, hidden : 2 * hidden]) + dot(
            hot, vals[:, 2 * hidden : 3 * hidden]
        )
        acc[here, 2 * hidden :] += dot(hot, vals[:, 3 * hidden :])

    for s in range(subs):
        block = step * subs + s
        following = jnp.where(block + 1 < steps * subs, block + 1, 0)
        gather(following, bufs[(s + 1) % 2])
        wide = lax.broadcasted_iota(jnp.int16, (LANES, LANES), 1)
        highs = []
        for c, place in enumerate(columns_of(perm_col, block * lines)):
            low = i16(jnp.broadcast_to(place & (ROWS_EL - 1), (LANES, LANES)))
            highs.append(jnp.broadcast_to(place >> (ROWS_EL.bit_length() - 1), (LANES, hidden)))
            for t in range(ROWS_EL // LANES):
                pick[c * LANES : (c + 1) * LANES, t * LANES : (t + 1) * LANES] = onehot(
                    low == wide + jnp.int16(t * LANES)
                )
        found = dot(pick[...], spread_feat[...])
        high = jnp.concatenate(highs, 0)
        lane = lax.broadcasted_iota(i32, (SUB, hidden), 1)
        found = jnp.where((lane & 15) == high, found, 0.0).astype(bf16)
        select = lax.broadcasted_iota(i32, (16, hidden), 1) >> 4
        select = onehot(select == lax.broadcasted_iota(i32, (16, hidden), 0))
        feat_out[:, s * SUB : (s + 1) * SUB] = dot_nt(select, found).astype(bf16)
        embed = dot(found, w_edge_rep[...]).astype(bf16)
        m = get_rows(bufs[s % 2], SUB) + dot(embed, w_pre[2 * hidden :, :]) + b_pre[...]
        spot = lax.broadcasted_iota(i32, (SUB, hidden), 0) + block * SUB
        m = jnp.where(spot < edge_live[0], m, 0.0)
        m_out[s * SUB : (s + 1) * SUB, :] = m
        low = m.astype(bf16)
        vals[:, :hidden] = low
        wide_low = low.astype(f32)
        square = wide_low * wide_low
        top = square.astype(bf16)
        vals[:, hidden : 2 * hidden] = top
        vals[:, 2 * hidden : 3 * hidden] = (square - top.astype(f32)).astype(bf16)
        vals[:, 3 * hidden : 4 * hidden] = jnp.exp(m).astype(bf16)
        vals[:, 4 * hidden :] = jnp.exp(-m).astype(bf16)
        base, windows = window_of(dst_idx, block * lines)
        add_window(base, block)

        @pl.loop(1, windows)
        def _(w):
            add_window(base + w * WIN, block)


def forward_edges(sorted_edges, edge_count, table, edge_feat, w_edge, w_pre, b_pre, nodes):
    perm_col, dst_col, dst_row, dst_idx, src_idx = sorted_edges
    edges = edge_feat.shape[1]
    hidden = w_pre.shape[1]
    ext = table.shape[0]
    spread_feat = edge_feat.reshape(-1, ROWS_EL).T
    w_edge_rep = jnp.repeat(w_edge, edges // ROWS_EL, axis=0)
    step_edges = 1024
    steps = edges // step_edges
    whole = lambda *shape: pl.BlockSpec(shape, lambda i: (0,) * len(shape))
    return pl.pallas_call(
        forward_kernel,
        grid=(steps,),
        out_shape=[
            jax.ShapeDtypeStruct((edges, hidden), f32),
            jax.ShapeDtypeStruct((16, edges), bf16),
            jax.ShapeDtypeStruct((nodes + WIN, 4 * hidden), f32),
            jax.ShapeDtypeStruct((nodes + WIN, LANES), f32),
        ],
        in_specs=[
            SMEM,
            SMEM,
            SMEM,
            whole(ext, hidden),
            whole(ROWS_EL, hidden),
            whole(LANES, LANES),
            whole(edges // SUB, SUB // LANES, LANES),
            whole(3 * hidden, hidden),
            whole(hidden, hidden),
            whole(1, hidden),
        ],
        out_specs=[
            pl.BlockSpec((step_edges, hidden), lambda i: (i, 0)),
            pl.BlockSpec((16, step_edges), lambda i: (0, i)),
            whole(nodes + WIN, 4 * hidden),
            whole(nodes + WIN, LANES),
        ],
        scratch_shapes=[
            pltpu.VMEM((ext, 2, LANES), f32),
            pltpu.VMEM((nodes, 2, LANES), f32),
            pltpu.VMEM((SUB, 2, LANES), f32),
            pltpu.VMEM((SUB, 2, LANES), f32),
            pltpu.VMEM((SUB, ROWS_EL), bf16),
            pltpu.VMEM((SUB, 5 * hidden), bf16),
        ],
        compiler_params=params(),
        name="forward_edges",
    )(
        src_idx,
        dst_idx,
        edge_count,
        table,
        spread_feat,
        perm_col,
        dst_row.reshape(edges // SUB, SUB // LANES, LANES),
        w_pre,
        w_edge_rep,
        b_pre.reshape(1, hidden),
    )


CHAINS = 4


def backward_kernel(
    src_idx,
    dst_idx,
    m_in,
    feat,
    dst_col,
    dst_row,
    weights,
    dst_grad,
    src_grad,
    feat_sum,
    bias_grad,
    dst_sum,
    acc0,
    acc1,
    acc2,
    acc3,
    rows_a,
    rows_b,
    got,
    low,
):
    step = pl.program_id(0)
    steps = pl.num_programs(0)
    subs = m_in.shape[0] // SUB
    lines = SUB // LANES
    hidden = m_in.shape[1]
    accs = [acc0, acc1, acc2, acc3]
    bufs = [rows_a, rows_b]

    @pl.when(step == 0)
    def _():
        for ref in accs + bufs:
            ref[...] = jnp.zeros_like(ref)
        dst_sum[...] = jnp.zeros_like(dst_sum)
        feat_sum[...] = jnp.zeros_like(feat_sum)

    def scatter(block, rows):
        for j in range(SUB):
            into = flat(accs[j % CHAINS])
            at = pl.ds(src_idx[block * lines + j // LANES, j % LANES], 2)
            into[at, :] = into[at, :] + flat(rows)[pl.ds(2 * j, 2), :]

    def take_window(block, base, more):
        wide = lax.broadcasted_iota(jnp.int16, (LANES, WIN), 1)
        hot = []
        for place in columns_of(dst_col, block * lines):
            hot.append(onehot(i16(jnp.broadcast_to(place - base, (LANES, WIN))) == wide))
        hot = jnp.concatenate(hot, 0)
        here = pl.ds(pl.multiple_of(base, 16), WIN)
        for q in range(4):
            part = dot(hot, weights[here, q * hidden : (q + 1) * hidden])
            if q == 0:
                part = part + dot(hot, weights[here, 4 * hidden :])
            to = slice(q * hidden, (q + 1) * hidden)
            got[:, to] = got[:, to] + part if more else part

    def add_window(block, base):
        hot = jnp.concatenate(target_rows(dst_row, block, base), 1)
        dst_sum[pl.ds(pl.multiple_of(base, 8), WIN), :] += dot(hot, low[...])

    for s in range(subs):
        block = step * subs + s
        scatter(jnp.maximum(block - 1, 0), bufs[(s + 1) % 2])
        base, windows = window_of(dst_idx, block * lines)
        take_window(block, base, False)

        @pl.loop(1, windows)
        def _(w):
            take_window(block, base + w * WIN, True)

        m = m_in[s * SUB : (s + 1) * SUB, :]
        grad = (
            got[:, :hidden]
            + got[:, hidden : 2 * hidden] * m.astype(bf16).astype(f32)
            + got[:, 2 * hidden : 3 * hidden] * jnp.exp(m).astype(bf16).astype(f32)
            + got[:, 3 * hidden : 4 * hidden] * jnp.exp(-m).astype(bf16).astype(f32)
        ).astype(bf16)
        low[...] = grad
        put_rows(bufs[s % 2], 0, grad.astype(f32))
        feat_sum[...] += dot(feat[:, s * SUB : (s + 1) * SUB], low[...])
        add_window(block, base)

        @pl.loop(1, windows)
        def _(w):
            add_window(block, base + w * WIN)

    @pl.when(step == steps - 1)
    def _():
        scatter(steps * subs - 1, bufs[(subs - 1) % 2])

        @pl.loop(0, src_grad.shape[0] // 256)
        def _(c):
            at = pl.multiple_of(c * 256, 256)
            for j in range(2):
                here = pl.ds(2 * at + j, 256, stride=2)
                src_grad[pl.ds(at, 256), j * LANES : (j + 1) * LANES] = (
                    (flat(acc0)[here, :] + flat(acc1)[here, :])
                    + (flat(acc2)[here, :] + flat(acc3)[here, :])
                ).astype(bf16)

        bias_grad[...] = jnp.zeros_like(bias_grad)

        @pl.loop(0, dst_grad.shape[0] // 256)
        def _(c):
            here = pl.ds(pl.multiple_of(c * 256, 256), 256)
            part = dst_sum[here, :]
            dst_grad[here, :] = part.astype(bf16)
            bias_grad[...] += jnp.sum(part, 0, keepdims=True)


def backward_edges(sorted_edges, messages, feat, weights, ext):
    perm_col, dst_col, dst_row, dst_idx, src_idx = sorted_edges
    edges, hidden = messages.shape
    padded = weights.shape[0]
    step_edges = 2 * SUB
    whole = lambda *shape: pl.BlockSpec(shape, lambda i: (0,) * len(shape))
    return pl.pallas_call(
        backward_kernel,
        grid=(edges // step_edges,),
        out_shape=[
            jax.ShapeDtypeStruct((padded - WIN, hidden), bf16),
            jax.ShapeDtypeStruct((ext, hidden), bf16),
            jax.ShapeDtypeStruct((16, hidden), f32),
            jax.ShapeDtypeStruct((1, hidden), f32),
        ],
        in_specs=[
            SMEM,
            SMEM,
            pl.BlockSpec((step_edges, hidden), lambda i: (i, 0)),
            pl.BlockSpec((16, step_edges), lambda i: (0, i)),
            whole(LANES, LANES),
            whole(edges // SUB, SUB // LANES, LANES),
            whole(padded, 5 * hidden),
        ],
        out_specs=[
            whole(padded - WIN, hidden),
            whole(ext, hidden),
            whole(16, hidden),
            whole(1, hidden),
        ],
        scratch_shapes=[pltpu.VMEM((padded, hidden), f32)]
        + [pltpu.VMEM((ext, 2, LANES), f32)] * CHAINS
        + [pltpu.VMEM((SUB, 2, LANES), f32)] * 2
        + [pltpu.VMEM((SUB, 4 * hidden), f32), pltpu.VMEM((SUB, hidden), bf16)],
        compiler_params=params(),
        name="backward_edges",
    )(
        src_idx,
        dst_idx,
        messages,
        feat,
        dst_col,
        dst_row.reshape(edges // SUB, SUB // LANES, LANES),
        weights,
    )


MESH = pl.DeviceIdType.MESH


def low_count(regions):
    bits = regions.bit_length() - 1
    return 1 << ((bits + 1) // 2)


def all_sum_kernel(n_low, n_high, x, out, buf1, buf2, send1, recv1, send2, recv2):
    region, grp = lax.axis_index("region"), lax.axis_index("grp")
    low, high = lax.rem(region, n_low), region // n_low
    n1 = 2 * n_low
    me1, me2 = low * 2 + grp, high

    def peer1(k):
        p = lax.rem(me1 + k, n1)
        return p, (high * n_low + p // 2, lax.rem(p, 2))

    def peer2(k):
        p = lax.rem(me2 + k, n_high)
        return p, (p * n_low + low, grp)

    barrier = pltpu.get_barrier_semaphore()
    for k in range(1, n1):
        pl.semaphore_signal(barrier, inc=1, device_id=peer1(k)[1], device_id_type=MESH)
    for k in range(1, n_high):
        pl.semaphore_signal(barrier, inc=1, device_id=peer2(k)[1], device_id_type=MESH)
    pl.semaphore_wait(barrier, n1 + n_high - 2)

    def stage(count, me, peer, buf, send, recv):
        copies = []
        for k in range(1, count):
            copy = pltpu.make_async_remote_copy(
                src_ref=buf.at[me],
                dst_ref=buf.at[me],
                send_sem=send.at[k],
                recv_sem=recv.at[me],
                device_id=peer(k)[1],
                device_id_type=MESH,
            )
            copy.start()
            copies.append(copy)
        for k in range(1, count):
            p, where = peer(k)
            pltpu.make_async_remote_copy(
                src_ref=buf.at[p],
                dst_ref=buf.at[p],
                send_sem=send.at[k],
                recv_sem=recv.at[p],
                device_id=where,
                device_id_type=MESH,
            ).wait_recv()
        for copy in copies:
            copy.wait_send()
        total = buf[0]
        for i in range(1, count):
            total = total + buf[i]
        return total

    buf1[me1] = x[...]
    buf2[me2] = stage(n1, me1, peer1, buf1, send1, recv1)
    out[...] = stage(n_high, me2, peer2, buf2, send2, recv2)


def all_sum(x, collective_id):
    regions = lax.axis_size("region")
    n_low = low_count(regions)
    n_high = regions // n_low
    dma = pltpu.SemaphoreType.DMA
    return pl.pallas_call(
        functools.partial(all_sum_kernel, n_low, n_high),
        out_shape=jax.ShapeDtypeStruct(x.shape, x.dtype),
        in_specs=[VMEM],
        out_specs=VMEM,
        scratch_shapes=[
            pltpu.VMEM((2 * n_low,) + x.shape, x.dtype),
            pltpu.VMEM((n_high,) + x.shape, x.dtype),
            dma((2 * n_low,)),
            dma((2 * n_low,)),
            dma((n_high,)),
            dma((n_high,)),
        ],
        compiler_params=pltpu.CompilerParams(
            collective_id=collective_id, has_side_effects=True
        ),
        name="all_sum_%d" % collective_id,
    )(x)


avg_log_degree = 2.2
norm_eps = 1e-05
CHUNK = 256


def live_mask(node_live, step, width):
    spot = lax.broadcasted_iota(i32, (CHUNK, width), 0) + step * CHUNK
    return jnp.where(spot < node_live[0], 1.0, 0.0)


def aggregates(acc, deg):
    hidden = acc.shape[1] // 4
    degree = jnp.sum(deg[...], 1, keepdims=True)
    clamped = jnp.maximum(degree, 1.0)
    log_count = jnp.log(degree + 1.0)
    amplify = log_count / avg_log_degree
    attenuate = avg_log_degree / jnp.log(clamped + 1.0)
    share = 1.0 / clamped
    mean = acc[:, :hidden] / clamped
    square = acc[:, hidden : 2 * hidden] / clamped
    spread = jnp.sqrt(jnp.maximum(square - mean * mean, 0.0) + 1.0)
    up = acc[:, 2 * hidden : 3 * hidden] + 1.0
    down = acc[:, 3 * hidden :] + 1.0
    soft_max = jnp.log(up) - log_count
    soft_min = log_count - jnp.log(down)
    return (mean, soft_max, soft_min, spread), (None, amplify, attenuate), share, up, down


def scaled(value, scale):
    return (value if scale is None else value * scale).astype(bf16)


def spread_towers(w_post_agg, towers_w):
    hidden = w_post_agg.shape[1]
    width = hidden // TOWERS
    row = lax.broadcasted_iota(i32, (hidden, hidden), 0) // width
    col = lax.broadcasted_iota(i32, (hidden, hidden), 1) // width
    for k in range(12):
        part = w_post_agg[k * width : (k + 1) * width, :]
        tall = jnp.concatenate([part] * TOWERS, 0).astype(f32)
        towers_w[k] = jnp.where(row == col, tall, 0.0).astype(bf16)


def node_forward_kernel(
    node_live, acc, deg, node_feat, w_post_x, w_post_agg, w_lin, post, lin, stats, towers_w
):
    step = pl.program_id(0)

    @pl.when(step == 0)
    def _():
        spread_towers(w_post_agg, towers_w)
        stats[...] = jnp.zeros_like(stats)

    parts, scales, _, _, _ = aggregates(acc, deg)
    total = dot(node_feat[...], w_post_x[...])
    for s in range(3):
        for a in range(4):
            total = total + dot(scaled(parts[a], scales[s]), towers_w[4 * s + a])
    post[...] = total.astype(bf16)
    out = dot(post[...], w_lin[...])
    lin[...] = out
    mask = live_mask(node_live, step, out.shape[1])
    masked = out * mask
    stats[0:1, :] += jnp.sum(masked, 0, keepdims=True)
    stats[1:2, :] += jnp.sum(masked * out, 0, keepdims=True)
    stats[2:3, :] += jnp.sum(mask, 0, keepdims=True)


def whole_spec(*shape):
    return pl.BlockSpec(shape, lambda i: (0,) * len(shape))


def chunk_spec(width, rows=CHUNK):
    return pl.BlockSpec((rows, width), lambda i: (i, 0))


def node_forward(node_count, acc, deg, node_feat, w_post_x, w_post_agg, w_lin):
    nodes, hidden = node_feat.shape
    return pl.pallas_call(
        node_forward_kernel,
        grid=(nodes // CHUNK,),
        out_shape=[
            jax.ShapeDtypeStruct((nodes, hidden), bf16),
            jax.ShapeDtypeStruct((nodes, hidden), f32),
            jax.ShapeDtypeStruct((8, hidden), f32),
        ],
        in_specs=[
            SMEM,
            chunk_spec(4 * hidden),
            chunk_spec(LANES),
            chunk_spec(hidden),
            whole_spec(hidden, hidden),
            whole_spec(3 * hidden, hidden),
            whole_spec(hidden, hidden),
        ],
        out_specs=[chunk_spec(hidden), chunk_spec(hidden), whole_spec(8, hidden)],
        scratch_shapes=[pltpu.VMEM((12, hidden, hidden), bf16)],
        compiler_params=params(),
        name="node_forward",
    )(node_count, acc, deg, node_feat, w_post_x, w_post_agg, w_lin)


SLOPE = 0.7978845608028654
CUBE = 0.044715


def norm_of(stats, lin, norm):
    count = stats[2:3, :]
    centre = stats[0:1, :] / count
    inverse = lax.rsqrt(stats[1:2, :] / count - centre * centre + norm_eps)
    normed = (lin[...] - centre) * inverse
    return normed, normed * norm[0:1, :] + norm[1:2, :], inverse, count


def gelu_parts(v):
    half = 0.5 * (1.0 + jnp.tanh(SLOPE * (v + CUBE * v * v * v)))
    slope = half + v * 2.0 * half * (1.0 - half) * SLOPE * (1.0 + 3.0 * CUBE * v * v)
    return v * half, slope


def node_middle_kernel(node_live, stats, norm, lin, node_feat, out_grad, output, sums):
    step = pl.program_id(0)

    @pl.when(step == 0)
    def _():
        sums[...] = jnp.zeros_like(sums)

    normed, shifted, _, _ = norm_of(stats, lin, norm)
    mask = live_mask(node_live, step, lin.shape[1])
    value, slope = gelu_parts(shifted)
    output[...] = (node_feat[...].astype(f32) + mask * value).astype(bf16)
    grad = out_grad[...].astype(f32) * mask * slope
    sums[0:1, :] += jnp.sum(grad, 0, keepdims=True)
    sums[1:2, :] += jnp.sum(grad * normed, 0, keepdims=True)


def node_middle(node_count, stats, norm, lin, node_feat, out_grad):
    nodes, hidden = node_feat.shape
    return pl.pallas_call(
        node_middle_kernel,
        grid=(nodes // CHUNK,),
        out_shape=[
            jax.ShapeDtypeStruct((nodes, hidden), bf16),
            jax.ShapeDtypeStruct((8, hidden), f32),
        ],
        in_specs=[SMEM, whole_spec(8, hidden), whole_spec(2, hidden)] + [chunk_spec(hidden)] * 3,
        out_specs=[chunk_spec(hidden), whole_spec(8, hidden)],
        compiler_params=params(),
        name="node_middle",
    )(node_count, stats, norm, lin, node_feat, out_grad)


def node_backward_kernel(
    node_live,
    stats,
    sums,
    norm,
    acc,
    deg,
    lin,
    post,
    node_feat,
    out_grad,
    w_post_x,
    w_post_agg,
    w_lin,
    weights,
    input_grad,
    w_lin_grad,
    w_post_x_grad,
    w_agg_grad,
    towers_w,
    agg_sum,
):
    step = pl.program_id(0)
    hidden = lin.shape[1]

    @pl.when(step == 0)
    def _():
        spread_towers(w_post_agg, towers_w)
        weights[pl.ds(lin.shape[0] * pl.num_programs(0), WIN), :] = jnp.zeros((WIN, 5 * hidden), bf16)
        w_lin_grad[...] = jnp.zeros_like(w_lin_grad)
        w_post_x_grad[...] = jnp.zeros_like(w_post_x_grad)
        agg_sum[...] = jnp.zeros_like(agg_sum)

    normed, shifted, inverse, count = norm_of(stats, lin, norm)
    mask = live_mask(node_live, step, hidden)
    upstream = out_grad[...].astype(f32)
    shift_grad = upstream * mask * gelu_parts(shifted)[1]
    lin_grad = (
        mask
        * inverse
        * norm[0:1, :]
        * (shift_grad - sums[0:1, :] / count - normed * (sums[1:2, :] / count))
    ).astype(bf16)
    post_grad = dot_nt(lin_grad, w_lin[...]).astype(bf16)
    w_lin_grad[...] += dot_tn(post[...], lin_grad)
    w_post_x_grad[...] += dot_tn(node_feat[...], post_grad)
    input_grad[...] = upstream + dot_nt(post_grad, w_post_x[...])
    parts, scales, share, up, down = aggregates(acc, deg)
    turned = post_grad.T
    grads = []
    for a in range(4):
        grad = None
        for s in range(3):
            k = 4 * s + a
            agg_sum[k] += dot(turned, scaled(parts[a], scales[s]))
            piece = dot_nt(post_grad, towers_w[k])
            piece = piece if s == 0 else piece * scales[s]
            grad = piece if grad is None else grad + piece
        grads.append(grad)
    mean, _, _, spread = parts
    ws = (grads[3] / spread * share).astype(bf16)
    wu, wd = grads[1] / up, grads[2] / down
    wu_low, wd_low = wu.astype(bf16), wd.astype(bf16)
    wm = grads[0] - ws.astype(f32) * mean / share
    wm = wm + (wu - wu_low.astype(f32)) * (up - 1.0) + (wd - wd_low.astype(f32)) * (down - 1.0)
    wm = wm * share
    wm_low = wm.astype(bf16)
    here = pl.ds(pl.multiple_of(step * CHUNK, CHUNK), CHUNK)
    wm_rest = (wm - wm_low.astype(f32)).astype(bf16)
    for q, value in enumerate((wm_low, ws, wu_low, wd_low, wm_rest)):
        weights[here, q * hidden : (q + 1) * hidden] = value

    @pl.when(step == pl.num_programs(0) - 1)
    def _():
        width = hidden // TOWERS
        row = lax.broadcasted_iota(i32, (hidden, hidden), 0) // width
        col = lax.broadcasted_iota(i32, (hidden, hidden), 1) // width
        for k in range(12):
            block = jnp.where(row == col, agg_sum[k], 0.0).T
            total = block[:width]
            for t in range(1, TOWERS):
                total = total + block[t * width : (t + 1) * width]
            w_agg_grad[k * width : (k + 1) * width, :] = total


def node_backward(
    node_count, stats, sums, norm, acc, deg, lin, post, node_feat, out_grad, w_post_x, w_post_agg, w_lin
):
    nodes, hidden = node_feat.shape
    return pl.pallas_call(
        node_backward_kernel,
        grid=(nodes // CHUNK,),
        out_shape=[
            jax.ShapeDtypeStruct((nodes + WIN, 5 * hidden), bf16),
            jax.ShapeDtypeStruct((nodes, hidden), f32),
            jax.ShapeDtypeStruct((hidden, hidden), f32),
            jax.ShapeDtypeStruct((hidden, hidden), f32),
            jax.ShapeDtypeStruct((3 * hidden, hidden), f32),
        ],
        in_specs=[
            SMEM,
            whole_spec(8, hidden),
            whole_spec(8, hidden),
            whole_spec(2, hidden),
            chunk_spec(4 * hidden),
            chunk_spec(LANES),
            chunk_spec(hidden),
            chunk_spec(hidden),
            chunk_spec(hidden),
            chunk_spec(hidden),
            whole_spec(hidden, hidden),
            whole_spec(3 * hidden, hidden),
            whole_spec(hidden, hidden),
        ],
        out_specs=[
            whole_spec(nodes + WIN, 5 * hidden),
            chunk_spec(hidden),
            whole_spec(hidden, hidden),
            whole_spec(hidden, hidden),
            whole_spec(3 * hidden, hidden),
        ],
        scratch_shapes=[
            pltpu.VMEM((12, hidden, hidden), bf16),
            pltpu.VMEM((12, hidden, hidden), f32),
        ],
        compiler_params=params(),
        name="node_backward",
    )(
        node_count,
        stats,
        sums,
        norm,
        acc,
        deg,
        lin,
        post,
        node_feat,
        out_grad,
        w_post_x,
        w_post_agg,
        w_lin,
    )


def finish_kernel(
    n_low,
    n_high,
    grads,
    exact,
    halo,
    total,
    exact_total,
    returned,
    own,
    half_in,
    low_out,
    low_in,
    high_out,
    high_in,
    gathered,
    ex1,
    ex2,
    halo_sem,
    send0,
    recv0,
    send1,
    recv1,
    send2,
    recv2,
    send3,
    recv3,
    send4,
    recv4,
    send5,
    recv5,
    xs1,
    xr1,
    xs2,
    xr2,
):
    region, grp = lax.axis_index("region"), lax.axis_index("grp")
    regions = n_low * n_high
    low, high = lax.rem(region, n_low), region // n_low
    n1 = 2 * n_low
    me1 = low * 2 + grp
    pair = halo.shape[0] // 2
    side = pair // 2
    partner = (region, 1 - grp)

    def near(k):
        p = lax.rem(me1 + k, n1)
        return p, (high * n_low + p // 2, lax.rem(p, 2))

    def flat_peer(k):
        p = lax.rem(low + k, n_low)
        return p, (high * n_low + p, grp)

    def tall_peer(k):
        p = lax.rem(high + k, n_high)
        return p, (p * n_low + low, grp)

    def remote(src, dst, send, recv, where):
        return pltpu.make_async_remote_copy(
            src_ref=src,
            dst_ref=dst,
            send_sem=send,
            recv_sem=recv,
            device_id=where,
            device_id_type=MESH,
        )

    barrier = pltpu.get_barrier_semaphore()

    def greet(where):
        pl.semaphore_signal(barrier, inc=1, device_id=where, device_id_type=MESH)

    for k in range(1, n1):
        greet(near(k)[1])
    for k in range(1, n_high):
        greet(tall_peer(k)[1])

    @pl.when(region > 0)
    def _():
        greet((region - 1, grp))

    @pl.when(region < regions - 1)
    def _():
        greet((region + 1, grp))

    own[...] = grads[...].astype(bf16)
    ex1[me1] = exact[...]
    neighbours = jnp.where(region > 0, 1, 0) + jnp.where(region < regions - 1, 1, 0)
    pl.semaphore_wait(barrier, n1 + n_high - 2 + neighbours)
    first = remote(own.at[1 - grp], half_in, send0, recv0, partner)
    first.start()

    def all_start(count, me, peer, buf, send, recv):
        copies = []
        for k in range(1, count):
            copy = remote(buf.at[me], buf.at[me], send.at[k], recv.at[me], peer(k)[1])
            copy.start()
            copies.append(copy)
        return copies

    def all_wait(count, peer, buf, send, recv, copies):
        for k in range(1, count):
            p, where = peer(k)
            remote(buf.at[p], buf.at[p], send.at[k], recv.at[p], where).wait_recv()
        for copy in copies:
            copy.wait_send()

    ex_copies = all_start(n1, me1, near, ex1, xs1, xr1)
    to_pair = remote(
        halo.at[pl.ds(0, pair)], returned.at[pl.ds(0, pair)], halo_sem.at[0], halo_sem.at[1], partner
    )
    to_pair.start()
    to_lower = remote(
        halo.at[pl.ds(pair, side)],
        returned.at[pl.ds(pair + side, side)],
        halo_sem.at[2],
        halo_sem.at[3],
        (region - 1, grp),
    )
    to_upper = remote(
        halo.at[pl.ds(pair + side, side)],
        returned.at[pl.ds(pair, side)],
        halo_sem.at[4],
        halo_sem.at[5],
        (region + 1, grp),
    )

    @pl.when(region > 0)
    def _():
        to_lower.start()

    @pl.when(region < regions - 1)
    def _():
        to_upper.start()

    def scatter_start(count, me, peer, out, into, send, recv):
        copies = []
        for k in range(1, count):
            p, where = peer(k)
            copy = remote(out.at[p], into.at[me], send.at[k], recv.at[me], where)
            copy.start()
            copies.append(copy)
        return copies

    def scatter_wait(count, peer, out, into, send, recv, copies):
        for k in range(1, count):
            p, where = peer(k)
            remote(out.at[p], into.at[p], send.at[k], recv.at[p], where).wait_recv()
        for copy in copies:
            copy.wait_send()

    def tree(values):
        while len(values) > 1:
            values = [a + b for a, b in zip(values[::2], values[1::2])]
        return values[0]

    first.wait()
    low_out[...] = (grads[grp] + half_in[...].astype(f32)).astype(bf16)
    copies = scatter_start(n_low, low, flat_peer, low_out, low_in, send1, recv1)
    low_in[low] = low_out[low]
    all_wait(n1, near, ex1, xs1, xr1, ex_copies)
    ex2[high] = tree([ex1[i] for i in range(n1)])
    ex_copies = all_start(n_high, high, tall_peer, ex2, xs2, xr2)
    scatter_wait(n_low, flat_peer, low_out, low_in, send1, recv1, copies)
    high_out[...] = tree([low_in[i].astype(f32) for i in range(n_low)]).astype(bf16)
    copies = scatter_start(n_high, high, tall_peer, high_out, high_in, send2, recv2)
    high_in[high] = high_out[high]
    scatter_wait(n_high, tall_peer, high_out, high_in, send2, recv2, copies)
    gathered[grp, low, high] = tree([high_in[i].astype(f32) for i in range(n_high)]).astype(bf16)

    part = gathered.at[grp, low]
    copies = all_start(n_high, high, tall_peer, part, send3, recv3)
    all_wait(n_high, tall_peer, ex2, xs2, xr2, ex_copies)
    exact_total[...] = tree([ex2[i] for i in range(n_high)])
    all_wait(n_high, tall_peer, part, send3, recv3, copies)
    part = gathered.at[grp]
    copies = all_start(n_low, low, flat_peer, part, send4, recv4)
    all_wait(n_low, flat_peer, part, send4, recv4, copies)
    last = remote(gathered.at[grp], gathered.at[grp], send5, recv5, partner)
    last.start()
    total[grp] = gathered[grp].astype(f32)
    to_pair.wait()

    @pl.when(region > 0)
    def _():
        to_lower.wait_send()

    @pl.when(region < regions - 1)
    def _():
        to_upper.wait_send()

    @pl.when(region > 0)
    def _():
        to_upper.wait_recv()

    @pl.when(region < regions - 1)
    def _():
        to_lower.wait_recv()

    @pl.when(region == 0)
    def _():
        returned[pl.ds(pair, side), :] = jnp.zeros((side, halo.shape[1]), bf16)

    @pl.when(region == regions - 1)
    def _():
        returned[pl.ds(pair + side, side), :] = jnp.zeros((side, halo.shape[1]), bf16)

    last.wait_send()
    remote(gathered.at[1 - grp], gathered.at[1 - grp], send5, recv5, partner).wait_recv()
    total[1 - grp] = gathered[1 - grp].astype(f32)


def finish(grads, exact, halo, collective_id):
    regions = lax.axis_size("region")
    n_low = low_count(regions)
    n_high = regions // n_low
    rows, hidden = grads.shape
    piece = rows // (2 * regions)
    shape = (2, n_low, n_high, piece, hidden)
    dma = pltpu.SemaphoreType.DMA
    total, exact_total, returned = pl.pallas_call(
        functools.partial(finish_kernel, n_low, n_high),
        out_shape=[
            jax.ShapeDtypeStruct(shape, f32),
            jax.ShapeDtypeStruct(exact.shape, f32),
            jax.ShapeDtypeStruct(halo.shape, bf16),
        ],
        in_specs=[VMEM] * 3,
        out_specs=[VMEM] * 3,
        scratch_shapes=[
            pltpu.VMEM(shape, bf16),
            pltpu.VMEM(shape[1:], bf16),
            pltpu.VMEM(shape[1:], bf16),
            pltpu.VMEM(shape[1:], bf16),
            pltpu.VMEM(shape[2:], bf16),
            pltpu.VMEM(shape[2:], bf16),
            pltpu.VMEM(shape, bf16),
            pltpu.VMEM((2 * n_low,) + exact.shape, f32),
            pltpu.VMEM((n_high,) + exact.shape, f32),
            dma((6,)),
            dma,
            dma,
            dma((n_low,)),
            dma((n_low,)),
            dma((n_high,)),
            dma((n_high,)),
            dma((n_high,)),
            dma((n_high,)),
            dma((n_low,)),
            dma((n_low,)),
            dma,
            dma,
            dma((2 * n_low,)),
            dma((2 * n_low,)),
            dma((n_high,)),
            dma((n_high,)),
        ],
        compiler_params=params(collective_id=collective_id, has_side_effects=True),
        name="finish",
    )(grads.reshape(shape), exact, halo)
    return total.reshape(rows, hidden), exact_total, returned


def from_partner(block, axis, stride):
    count = lax.axis_size(axis)
    route = []
    for low in range(count):
        high = low | 1 << stride
        if high != low and high < count:
            route += [(low, high), (high, low)]
    return lax.ppermute(block, axis, route)


def passed_along(value, axis, steps):
    count = lax.axis_size(axis)
    first, last = (max(0, -steps), min(count, count - steps))
    return lax.ppermute(value, axis, [(source, source + steps) for source in range(first, last)])


def per_device(
    node_feat,
    edge_feat,
    edge_src,
    edge_dst,
    send_rows,
    node_count,
    edge_count,
    w_edge,
    w_pre,
    b_pre,
    w_post_x,
    w_post_agg,
    w_lin,
    norm_gain,
    norm_bias,
    out_grad,
):
    nodes, hidden = node_feat.shape
    pair_size, side_size = nodes // 4, nodes // 8
    sent = jnp.take(node_feat, send_rows, axis=0)
    pair_in = from_partner(sent[:pair_size], "grp", 0)
    from_lower = passed_along(sent[pair_size + side_size :], "region", 1)
    from_upper = passed_along(sent[pair_size : pair_size + side_size], "region", -1)
    table = jnp.concatenate([node_feat, pair_in, from_lower, from_upper], 0)
    w_dst, w_src, w_edg = w_pre[:hidden], w_pre[hidden : 2 * hidden], w_pre[2 * hidden :]

    order = sort_edges(edge_dst, edge_src, edge_count, nodes)
    messages, feat, acc, deg = forward_edges(
        order, edge_count, table, edge_feat, w_edge, w_pre, b_pre, nodes
    )
    post, lin, stats = node_forward(
        node_count, acc, deg, node_feat, w_post_x, w_post_agg, w_lin
    )
    stats = all_sum(stats, 0)
    norm = jnp.stack([norm_gain, norm_bias])
    output, sums = node_middle(node_count, stats, norm, lin, node_feat, out_grad)
    sums = all_sum(sums, 1)
    weights, input_grad, w_lin_grad, w_post_x_grad, w_post_agg_grad = node_backward(
        node_count, stats, sums, norm, acc, deg, lin, post, node_feat, out_grad,
        w_post_x, w_post_agg, w_lin,
    )
    dst_grad, src_grad, feat_sum, bias = backward_edges(
        order, messages, feat, weights, table.shape[0]
    )
    high = lax.Precision.HIGHEST
    w_edg_grad = jnp.dot(w_edge.T.astype(f32), feat_sum, precision=high)
    w_edge_grad = jnp.dot(feat_sum, w_edg.T.astype(f32), precision=high)
    w_dst_grad = dot_tn(node_feat, dst_grad)
    w_src_grad = dot_tn(table, src_grad)
    input_grad = input_grad + dot_nt(dst_grad, w_dst) + dot_nt(src_grad[:nodes], w_src)
    grads = jnp.concatenate(
        [w_dst_grad, w_src_grad, w_edg_grad, w_post_x_grad, w_post_agg_grad, w_lin_grad], 0
    )
    exact = jnp.concatenate([w_edge_grad, bias, jnp.zeros((7, hidden), f32)], 0)
    total, exact, returned = finish(grads, exact, src_grad[nodes:], 2)
    place = (send_rows[None, :] == jnp.arange(nodes)[:, None]).astype(bf16)
    returned = dot(place, returned)
    top = returned.astype(bf16)
    rest = (returned - top.astype(f32)).astype(bf16)
    input_grad = input_grad + dot_nt(top, w_src) + dot_nt(rest, w_src)
    cuts = [3 * hidden, 4 * hidden, 7 * hidden]
    return (
        output,
        input_grad,
        exact[: w_edge.shape[0]],
        total[: cuts[0]],
        exact[w_edge.shape[0]],
        total[cuts[0] : cuts[1]],
        total[cuts[1] : cuts[2]],
        total[cuts[2] :],
        sums[1],
        sums[0],
    )


def solution(mesh):
    rows, lanes, flat_spec = P(("region", "grp"), None), P(None, ("region", "grp")), P(("region", "grp"))
    return jax.shard_map(
        per_device,
        mesh=mesh,
        in_specs=(rows, lanes) + (flat_spec,) * 5 + (P(),) * 8 + (rows,),
        out_specs=(rows, rows) + (P(),) * 8,
        check_vma=False,
    )
```
